512 devices in a mesh: user: 16 (over y, x), item: 32 (over z, core).
Axes of the slice: x: 4, y: 4, z: 16, core: 2. Of those that a mesh axis runs over, the one named last changes fastest.
Arguments:
- panel_users: bfloat16 [8192, 256], P(('user', 'item'))
- block_values: bfloat16 [8192, 224, 128], P('user', 'item')
- block_list: int32 [16, 224], P('user', 'item'), may hold values from 0 to 7, as said below
- block_count: int32 [16, 32], P('user', 'item'), may hold values from 1 to 7, as said below
Outputs:
- factor_diag: float32 [256, 256], replicated
- factor_below: float32 [32768, 256], P('item')
The draws below stay inside these ranges and needn't reach their ends.
Inputs may be any that keep to these rules, and one draw needn't show every extreme that they name: `block_list`: within one user shard and item index the first block_count slots name distinct row blocks. `block_count`: some device uses all slots.
All inputs are finite; a program needn't handle non-finite values.
Results may differ from the reference program's by a relative error of at most 0.0003.
Values may be sent and summed in bfloat16 or wider, within the bound.
A program may use at most 64 MiB of HBM per device.

```python
import jax
import jax.numpy as jnp
from jax import lax

BLOCK = 128
PANEL = 256
USERS_DEV = 512
BLK_DEV = 8
KMAX = 7
USERS = 8192
ROWS = 32768
N_USER = 16
N_ITEM = 32


def shared_draw(key):
    panel_key, list_key = jax.random.split(key)
    scale = USERS ** (-0.5)
    panel_full = scale * jax.random.normal(panel_key, (USERS, PANEL), jnp.float32)
    list_keys = jax.random.split(list_key, N_USER * N_ITEM)
    chosen = jax.vmap(lambda k: jax.random.permutation(k, BLK_DEV)[:KMAX])(list_keys)
    chosen = chosen.reshape(N_USER, N_ITEM * KMAX).astype(jnp.int32)
    return (panel_full, chosen)


def draw_panel_users(key, part):
    panel_full, chosen = shared_draw(key)
    return panel_full.astype(jnp.bfloat16)


def draw_block_list(key, part):
    panel_full, chosen = shared_draw(key)
    return chosen


def draw_block_values(key, part):
    panel_full, chosen = shared_draw(key)
    key = jax.random.fold_in(key, 13)
    scale = USERS ** (-0.5)
    item_of_slot = jnp.arange(N_ITEM * KMAX, dtype=jnp.int32) // KMAX
    global_block = chosen + BLK_DEV * item_of_slot[None, :]
    half = global_block % 2
    weight = 0.4 + 0.15 * (global_block * 7 % 5).astype(jnp.float32)
    half_rows = jnp.repeat(half, USERS_DEV, axis=0)
    weight_rows = jnp.repeat(weight, USERS_DEV, axis=0)
    panel_split = panel_full.reshape(USERS, 2, BLOCK)
    picked = jnp.where(half_rows[:, :, None] == 0, panel_split[:, None, 0, :], panel_split[:, None, 1, :])
    noise = scale * jax.random.normal(key, (USERS, N_ITEM * KMAX, BLOCK), jnp.float32)
    return (weight_rows[:, :, None] * picked + 0.7 * noise).astype(jnp.bfloat16)


def draw_block_count(key, part):
    key = jax.random.fold_in(key, 14)
    count_key, spot_key = jax.random.split(key)
    counted = jax.random.randint(count_key, (N_USER * N_ITEM,), 1, KMAX + 1)
    spot = jax.random.randint(spot_key, (), 0, N_USER * N_ITEM)
    counted = jnp.where(jnp.arange(N_USER * N_ITEM) == spot, KMAX, counted)
    return counted.reshape(N_USER, N_ITEM).astype(jnp.int32)


def setup_inputs(seed: int = 0) -> dict:
    key_list = jax.random.split(jax.random.key(seed), 5)
    return {
        "panel_users": draw_panel_users(jax.random.fold_in(key_list[4], 71), 0),
        "block_values": draw_block_values(jax.random.fold_in(key_list[4], 71), 0),
        "block_list": draw_block_list(jax.random.fold_in(key_list[4], 71), 0),
        "block_count": draw_block_count(jax.random.fold_in(key_list[4], 71), 0),
    }


def reference(panel_users, block_values, block_list, block_count):
    gram_diag = jnp.dot(panel_users.T.astype(jnp.float32), panel_users.astype(jnp.float32), preferred_element_type=jnp.float32)
    gram_diag = gram_diag + 0.5 * jnp.eye(PANEL, dtype=jnp.float32)
    blocks_here = jnp.arange(BLK_DEV, dtype=jnp.int32)
    slots_here = jnp.arange(KMAX, dtype=jnp.int32)

    def one_shard(total, shard):
        start = (shard * USERS_DEV).astype(jnp.int32)
        users_panel = lax.dynamic_slice_in_dim(panel_users, start, USERS_DEV, 0).astype(jnp.float32)
        users_blocks = lax.dynamic_slice_in_dim(block_values, start, USERS_DEV, 0).astype(jnp.float32)
        product = jnp.einsum('ukc,up->kcp', users_blocks, users_panel)
        product = product.reshape(N_ITEM, KMAX, BLOCK, PANEL)
        listed = block_list[shard].reshape(N_ITEM, KMAX)
        counted = block_count[shard]
        chosen = (listed[:, :, None] == blocks_here[None, None, :]) & (slots_here[None, :, None] < counted[:, None, None])
        placed = jnp.einsum('ikb,ikcp->ibcp', chosen.astype(jnp.float32), product)
        return (total + placed, None)
    start_total = jnp.zeros((N_ITEM, BLK_DEV, BLOCK, PANEL), jnp.float32)
    gram_below, _ = lax.scan(one_shard, start_total, jnp.arange(N_USER, dtype=jnp.int32))
    gram_below = gram_below.reshape(ROWS, PANEL)
    factor_diag = jnp.linalg.cholesky(gram_diag)
    factor_below = lax.linalg.triangular_solve(factor_diag, gram_below, left_side=False, lower=True, transpose_a=True)
    return (factor_diag, factor_below)
```

```python
import functools

import jax
import jax.numpy as jnp
from jax import lax
from jax.sharding import PartitionSpec as P
import jax.experimental.pallas as pl
import jax.experimental.pallas.tpu as pltpu

BLOCK = 128
PANEL = 256
BLK_DEV = 8
SIDE = 4
DEPTH = 16
SHARE = 16
NB = 16
MESH = pl.DeviceIdType.MESH
FAR_FIRST_Z = (8, 7, 9, 6, 10, 5, 11, 4, 12, 3, 13, 2, 14, 1, 15)
FAR_FIRST_XY = sorted(
    ((dy, dx) for dy in range(SIDE) for dx in range(SIDE) if dy or dx),
    key=lambda d: -(min(d[0], SIDE - d[0]) + min(d[1], SIDE - d[1])),
)
FAR_FIRST_SIDE = (2, 1, 3)


def split3(x):
    high = x.astype(jnp.bfloat16)
    rest = x - high.astype(jnp.float32)
    middle = rest.astype(jnp.bfloat16)
    low = (rest - middle.astype(jnp.float32)).astype(jnp.bfloat16)
    return high, middle, low


def eliminate(rows, sub, lane):
    tiles = len(rows)
    count = 8 * tiles
    columns = [
        [jnp.broadcast_to(rows[k][0][:, t : t + 1], (8, 128)) for k in range(tiles)] for t in range(count)
    ]
    inverse = [jnp.where(lane == sub + 8 * k, 1.0, 0.0).astype(jnp.float32) for k in range(tiles)]
    pivots = [None] * tiles
    for t in range(count):
        kt, s = divmod(t, 8)
        here = columns[t][kt]
        pivots[kt] = here if s == 0 else jnp.where(sub == s, here, pivots[kt])
        if t == count - 1:
            break
        reciprocal = 1.0 / jnp.broadcast_to(here[s : s + 1, :], (8, 128))
        below = {k: columns[t][k] for k in range(kt + 1, tiles)}
        if s < 7:
            below[kt] = jnp.where(sub > s, here, 0.0)
        for j in range(t + 1, count):
            pivot_row = jnp.broadcast_to(columns[j][kt][s : s + 1, :], (8, 128))
            for k in below:
                columns[j][k] = columns[j][k] - (below[k] * pivot_row) * reciprocal
        scaled = {k: below[k] * reciprocal for k in below}
        for h in range(len(rows[0])):
            pivot_row = jnp.broadcast_to(rows[kt][h][s : s + 1, :], (8, 128))
            for k in below:
                rows[k][h] = rows[k][h] - scaled[k] * pivot_row
        pivot_row = jnp.broadcast_to(inverse[kt][s : s + 1, :], (8, 128))
        for k in below:
            inverse[k] = inverse[k] - scaled[k] * pivot_row
    return rows, inverse, pivots


def factor_step(step, work_ref, upper_ref):
    tiles = NB // 8
    sub = lax.broadcasted_iota(jnp.int32, (8, 128), 0)
    lane = lax.broadcasted_iota(jnp.int32, (8, 128), 1)
    rows = [[work_ref[8 * k : 8 * k + 8, 128 * h : 128 * h + 128] for h in range(2)] for k in range(tiles)]
    rows, inverse, pivots = eliminate(rows, sub, lane)
    scale = [lax.rsqrt(p) for p in pivots]
    upper = jnp.concatenate(
        [jnp.concatenate([rows[k][h] * scale[k] for h in range(2)], 1) for k in range(tiles)], 0
    )
    inverse = jnp.concatenate([inverse[k] * scale[k] for k in range(tiles)], 0)
    inverse = jnp.concatenate([inverse, inverse], 1)
    col = lax.broadcasted_iota(jnp.int32, (NB, PANEL), 1)
    row = lax.broadcasted_iota(jnp.int32, (NB, PANEL), 0)
    left = PANEL - NB * step
    trailing = (col >= NB) & (col < left)
    done = jnp.where(col < NB, inverse, upper)
    into = jnp.where(trailing, upper, 0.0)
    upper_ref[pl.ds(pl.multiple_of(step * NB, NB), NB), :] = jnp.where((col >= row) & (col < left), upper, 0.0)
    dh, dm, dl = split3(done)
    ih, im, il = split3(into)
    product = lax.dot_general(
        jnp.concatenate([ih, ih, im, ih, im, il], 0),
        jnp.concatenate([dh, dm, dh, dl, dm, dh], 0),
        (((0,), (0,)), ((), ())),
        preferred_element_type=jnp.float32,
    )
    wide = lax.broadcasted_iota(jnp.int32, (PANEL - NB, PANEL), 1)
    new = jnp.where(wide < NB, 0.0, work_ref[NB:, :]) - product[NB:, :]
    work_ref[0 : PANEL - NB, :] = pltpu.roll(new, PANEL - NB, 1)
    work_ref[PANEL - NB :, :] = pltpu.roll(jnp.where(trailing, 0.0, done), PANEL - NB, 1)


def factor_steps(first, last, work_ref, upper_ref):
    def body(step, carry):
        factor_step(step, work_ref, upper_ref)
        return carry

    lax.fori_loop(first, last, body, 0)


def turn_back(upper_ref):
    def body(step, carry):
        rows = pl.ds(pl.multiple_of(step * NB, NB), NB)
        upper_ref[rows, :] = pltpu.roll(upper_ref[rows, :], step * NB, 1)
        return carry

    lax.fori_loop(0, PANEL // NB, body, 0)


def gram_kernel(
    panel_ref, values_ref, list_ref, count_ref, upper_ref, inverse_ref, sum_ref,
    users, values, turned, diag, diag_in, part, in1, sum1, in2,
    values_sem, z_send, z_recv, core_send, core_recv, ds_send, ds_recv, dg_send, dg_recv,
    s1_send, s1_recv, s2_send, s2_recv, s3_send, s3_recv, s4_send, s4_recv,
):
    user = lax.axis_index("user")
    item = lax.axis_index("item")
    y, x = user // SIDE, user % SIDE
    z, core = item // 2, item % 2
    other = 1 - core

    def at_xy(dy, dx):
        return ((y + dy) % SIDE) * SIDE + (x + dx) % SIDE

    def at_z(dz):
        return (z + dz) % DEPTH

    z_ids = [(user, at_z(d) * 2 + core) for d in FAR_FIRST_Z]
    xy_ids = [(at_xy(*d), item) for d in FAR_FIRST_XY]
    core_id = (user, z * 2 + other)

    def remote(src, dst, send, recv, device):
        return pltpu.make_async_remote_copy(
            src_ref=src, dst_ref=dst, send_sem=send, recv_sem=recv, device_id=device, device_id_type=MESH
        )

    barrier = pltpu.get_barrier_semaphore()
    for device in z_ids + xy_ids + [core_id]:
        pl.semaphore_signal(barrier, inc=1, device_id=device, device_id_type=MESH)

    loads = [
        pltpu.make_async_copy(
            values_ref.at[:, :, c], values.at[c, pl.ds(0, BLK_DEV - 1)], values_sem.at[c]
        )
        for c in range(2)
    ]
    for load in loads:
        load.start()
    for c in range(2):
        values[c, BLK_DEV - 1] = jnp.zeros((DEPTH, SHARE, BLOCK), jnp.bfloat16)
    users[core, z] = panel_ref[...]

    pl.semaphore_wait(barrier, len(z_ids) + len(xy_ids) + 1)

    z_copies = [
        remote(users.at[core, z], users.at[core, z], z_send.at[k], z_recv.at[k], device)
        for k, device in enumerate(z_ids)
    ]
    for copy in z_copies:
        copy.start()

    for load in loads:
        load.wait()
    used = count_ref[0, 0]
    for b in range(BLK_DEV):
        slot = jnp.int32(BLK_DEV - 1)
        for k in range(BLK_DEV - 1):
            slot = jnp.where((list_ref[0, k] == b) & (k < used), k, slot)
        for c in range(2):
            block = values[c, slot].reshape(DEPTH * SHARE, BLOCK)
            turned[c, pl.ds(b * BLOCK, BLOCK), :] = block.T

    for copy in z_copies:
        copy.wait()
    core_copy = remote(users.at[core], users.at[core], core_send, core_recv, core_id)
    core_copy.start()

    def partial(c):
        rows = users[c].reshape(DEPTH * SHARE, PANEL)
        return lax.dot_general(rows, rows, (((0,), (0,)), ((), ())), preferred_element_type=jnp.float32)

    diag[...] = partial(core)
    below = jnp.dot(
        turned[core], users[core].reshape(DEPTH * SHARE, PANEL), preferred_element_type=jnp.float32
    )
    part[0] = below[:, :BLOCK]
    part[1] = below[:, BLOCK:]
    core_copy.wait()
    diag[...] += partial(other)

    def diag_rows(device_user):
        return pl.ds(pl.multiple_of(device_user * SHARE, SHARE), SHARE)

    ds_copies = [
        remote(diag.at[diag_rows(d[0])], diag_in.at[user], ds_send.at[k], ds_recv.at[k], d)
        for k, d in enumerate(xy_ids)
    ]
    for copy in ds_copies:
        copy.start()
    diag_in[user] = diag[diag_rows(user), :]

    below = jnp.dot(
        turned[other], users[other].reshape(DEPTH * SHARE, PANEL), preferred_element_type=jnp.float32
    )
    part[0] += below[:, :BLOCK]
    part[1] += below[:, BLOCK:]

    along = (
        [((at_xy(0, d), item), (x + d) % SIDE) for d in FAR_FIRST_SIDE],
        [((at_xy(d, 0), item), (y + d) % SIDE) for d in FAR_FIRST_SIDE],
    )
    place = (x, y)
    big, small = BLK_DEV * BLOCK // SIDE, BLK_DEV * BLOCK // SIDE**2

    def big_rows(i):
        return pl.ds(pl.multiple_of(i * big, big), big)

    def small_rows(i):
        return pl.ds(pl.multiple_of(i * small, small), small)

    s1_copies = [
        remote(part.at[h, big_rows(there)], in1.at[h, k], s1_send.at[h, k], s1_recv.at[h, k], device)
        for k in range(SIDE - 1)
        for h in range(2)
        for device, there in [along[h][k]]
    ]
    for copy in s1_copies:
        copy.start()

    for copy in ds_copies:
        copy.wait()
    total = diag_in[0]
    for k in range(1, SIDE * SIDE):
        total = total + diag_in[k]
    row = lax.broadcasted_iota(jnp.int32, (SHARE, PANEL), 0) + user * SHARE
    col = lax.broadcasted_iota(jnp.int32, (SHARE, PANEL), 1)
    inverse_ref[diag_rows(user), :] = total + jnp.where(row == col, 0.5, 0.0)
    dg_copies = [
        remote(
            inverse_ref.at[diag_rows(user)], inverse_ref.at[diag_rows(user)], dg_send.at[k], dg_recv.at[k], d
        )
        for k, d in enumerate(xy_ids)
    ]
    for copy in dg_copies:
        copy.start()

    for copy in s1_copies:
        copy.wait()
    for h in range(2):
        sum1[h] = part[h, big_rows(place[h]), :] + in1[h, 0] + in1[h, 1] + in1[h, 2]
    s2_copies = [
        remote(sum1.at[h, small_rows(there)], in2.at[h, k], s2_send.at[h, k], s2_recv.at[h, k], device)
        for k in range(SIDE - 1)
        for h in range(2)
        for device, there in [along[1 - h][k]]
    ]
    for copy in s2_copies:
        copy.start()

    for copy in dg_copies:
        copy.wait()
    for copy in s2_copies:
        copy.wait()
    mine = (x * SIDE + y, y * SIDE + x)
    for h in range(2):
        sum_ref[h, small_rows(mine[h]), :] = (
            sum1[h, small_rows(place[1 - h]), :] + in2[h, 0] + in2[h, 1] + in2[h, 2]
        )
    s3_copies = [
        remote(
            sum_ref.at[h, small_rows(mine[h])], sum_ref.at[h, small_rows(mine[h])],
            s3_send.at[h, k], s3_recv.at[h, k], along[1 - h][k][0],
        )
        for k in range(SIDE - 1)
        for h in range(2)
    ]
    for copy in s3_copies:
        copy.start()
    factor_steps(0, 5, inverse_ref, upper_ref)
    for copy in s3_copies:
        copy.wait()
    s4_copies = [
        remote(
            sum_ref.at[h, big_rows(place[h])], sum_ref.at[h, big_rows(place[h])],
            s4_send.at[h, k], s4_recv.at[h, k], along[h][k][0],
        )
        for k in range(SIDE - 1)
        for h in range(2)
    ]
    for copy in s4_copies:
        copy.start()
    factor_steps(5, PANEL // NB, inverse_ref, upper_ref)
    turn_back(upper_ref)
    for copy in s4_copies:
        copy.wait()


def solve_kernel(upper_ref, inverse_ref, sum_ref, diag_ref, below_ref):
    diag_ref[...] = upper_ref[...].T
    rows = jnp.concatenate([sum_ref[0], sum_ref[1]], 1)
    below_ref[...] = lax.dot_general(
        rows, inverse_ref[...], (((1,), (1,)), ((), ())),
        precision=lax.Precision.HIGHEST, preferred_element_type=jnp.float32,
    )


def on_device(panel_users, block_values, block_list, block_count):
    f32, bf16 = jnp.float32, jnp.bfloat16
    rows = BLK_DEV * BLOCK
    big, small = rows // SIDE, rows // SIDE**2
    slots = block_values.shape[1]
    values = block_values.transpose(1, 0, 2).reshape(slots, DEPTH, 2, SHARE, BLOCK)
    vmem = pl.BlockSpec(memory_space=pltpu.VMEM)
    smem = pl.BlockSpec(memory_space=pltpu.SMEM)
    sems = pltpu.SemaphoreType.DMA
    xy = SIDE * SIDE - 1
    upper, inverse, total = pl.pallas_call(
        gram_kernel,
        out_shape=[
            jax.ShapeDtypeStruct((PANEL, PANEL), f32),
            jax.ShapeDtypeStruct((PANEL, PANEL), f32),
            jax.ShapeDtypeStruct((2, rows, BLOCK), f32),
        ],
        in_specs=[vmem, pl.BlockSpec(memory_space=pl.ANY), smem, smem],
        out_specs=[vmem, vmem, vmem],
        scratch_shapes=[
            pltpu.VMEM((2, DEPTH, SHARE, PANEL), bf16),
            pltpu.VMEM((2, BLK_DEV, DEPTH, SHARE, BLOCK), bf16),
            pltpu.VMEM((2, rows, 2 * BLOCK), bf16),
            pltpu.VMEM((PANEL, PANEL), f32),
            pltpu.VMEM((SIDE * SIDE, SHARE, PANEL), f32),
            pltpu.VMEM((2, rows, BLOCK), f32),
            pltpu.VMEM((2, SIDE - 1, big, BLOCK), f32),
            pltpu.VMEM((2, big, BLOCK), f32),
            pltpu.VMEM((2, SIDE - 1, small, BLOCK), f32),
            sems((2,)),
            sems((DEPTH - 1,)),
            sems((DEPTH - 1,)),
            sems,
            sems,
            sems((xy,)),
            sems((xy,)),
            sems((xy,)),
            sems((xy,)),
        ]
        + [sems((2, SIDE - 1))] * 8,
        compiler_params=pltpu.CompilerParams(
            collective_id=0, has_side_effects=True, vmem_limit_bytes=32 << 20
        ),
        name="gram",
    )(panel_users, values, block_list, block_count)
    return pl.pallas_call(
        solve_kernel,
        out_shape=[jax.ShapeDtypeStruct((PANEL, PANEL), f32), jax.ShapeDtypeStruct((rows, PANEL), f32)],
        in_specs=[vmem] * 3,
        out_specs=[vmem] * 2,
        compiler_params=pltpu.CompilerParams(vmem_limit_bytes=32 << 20),
        name="solve",
    )(upper, inverse, total)


def solution(mesh):
    in_specs = (
        P(("user", "item"), None),
        P("user", "item", None),
        P("user", "item"),
        P("user", "item"),
    )
    out_specs = (P(), P("item", None))
    return jax.shard_map(
        on_device, mesh=mesh, in_specs=in_specs, out_specs=out_specs, check_vma=False
    )
```

```python
import jax
import jax.numpy as jnp
from jax import lax
from jax.sharding import PartitionSpec as P
import jax.experimental.pallas as pl
import jax.experimental.pallas.tpu as pltpu

BLOCK = 128
PANEL = 256
BLK_DEV = 8
ROWS = BLK_DEV * BLOCK
SIDE = 4
DEPTH = 16
SHARE = 16
TILE = 8
NB = 32
STORES = 4
PIECES = 4
MESH = pl.DeviceIdType.MESH
FAR_FIRST_Z = (8, 7, 9, 6, 10, 5, 11, 4, 12, 3, 13, 2, 14, 1, 15)
FAR_FIRST_XY = sorted(
    ((dy, dx) for dy in range(SIDE) for dx in range(SIDE) if dy or dx),
    key=lambda d: -(min(d[0], SIDE - d[0]) + min(d[1], SIDE - d[1])),
)
FAR_FIRST_SIDE = (2, 1, 3)
ORDER = (
    ("sum", 0), ("sum", 1), ("diag", 0), ("factor", 0), ("sum", 2), ("factor", 1), ("sum", 3), ("pass", 0), ("factor", 2),
    ("pass", 1), ("factor", 3), ("pass", 2), ("factor", 4), ("pass", 3), ("factor", 5), ("factor", 6), ("factor", 7),
)


def split3(x):
    high = x.astype(jnp.bfloat16)
    rest = x - high.astype(jnp.float32)
    middle = rest.astype(jnp.bfloat16)
    low = (rest - middle.astype(jnp.float32)).astype(jnp.bfloat16)
    return high, middle, low


def eliminate(rows, inverse, start, count):
    left = rows.shape[0]
    columns = jnp.stack([jnp.broadcast_to(rows[:, start + t : start + t + 1], (left, BLOCK)) for t in range(count)])
    tile_sub = lax.broadcasted_iota(jnp.int32, (8, BLOCK), 0)
    rows_done, inverse_done, pivots = [], [], None
    for t in range(count):
        s = t % 8
        here = columns[0]
        pivots = jnp.where(tile_sub == s, here[:8], pivots) if s else here[:8]
        reciprocal = 1.0 / here[s : s + 1]
        below = jnp.where(lax.broadcasted_iota(jnp.int32, (left, BLOCK), 0) > s, here, 0.0)
        if t < count - 1:
            columns = columns[1:] - (below[None] * columns[1:, s : s + 1]) * reciprocal[None]
        scaled = below * reciprocal
        rows = rows - jnp.concatenate([scaled, scaled], 1) * rows[s : s + 1]
        inverse = inverse - scaled * inverse[s : s + 1]
        if s == 7:
            scale = lax.rsqrt(pivots)
            rows_done.append(rows[:8] * jnp.concatenate([scale, scale], 1))
            inverse_done.append(inverse[:8] * scale)
            left -= 8
            if left:
                rows, inverse, columns = rows[8:], inverse[8:], columns[:, 8:]
    return rows_done, inverse_done, rows, inverse


def factor_step(step, work_ref, upper_ref):
    start, stop = NB * step, NB * (step + 1)
    rows = work_ref[start:stop, :]
    lane = lax.broadcasted_iota(jnp.int32, (NB, BLOCK), 1)
    sub = lax.broadcasted_iota(jnp.int32, (NB, BLOCK), 0)
    inverse = jnp.where(lane == sub + start % BLOCK, 1.0, 0.0).astype(jnp.float32)
    rows1, inverse1, rows, inverse = eliminate(rows, inverse, start, NB // 2)
    rows2, inverse2, _, _ = eliminate(rows, inverse, start + NB // 2, NB // 2)
    upper = jnp.concatenate(rows1 + rows2, 0)
    inverse = jnp.concatenate(inverse1 + inverse2, 0)
    col = lax.broadcasted_iota(jnp.int32, (NB, PANEL), 1)
    row = lax.broadcasted_iota(jnp.int32, (NB, PANEL), 0)
    done = jnp.where((col >= start) & (col < stop), jnp.concatenate([inverse, inverse], 1), upper)
    upper_ref[start:stop, :] = jnp.where(col >= row + start, upper, 0.0)
    work_ref[start:stop, :] = jnp.where(col < stop, done, 0.0)
    if stop == PANEL:
        return
    base = BLOCK * (stop // BLOCK)
    dh, dm, dl = split3(done)
    ih, im, il = split3(upper[:, base:])
    product = lax.dot_general(
        jnp.concatenate([ih, ih, im, ih, im, il], 0),
        jnp.concatenate([dh, dm, dh, dl, dm, dh], 0),
        (((0,), (0,)), ((), ())),
        preferred_element_type=jnp.float32,
    )
    wide = lax.broadcasted_iota(jnp.int32, (PANEL - stop, PANEL), 1)
    kept = jnp.where((wide >= start) & (wide < stop), 0.0, work_ref[stop:, :])
    work_ref[stop:, :] = kept - product[stop - base :, :]


def gram_kernel(
    panel_ref, values_ref, list_ref, count_ref, diag_out, below_out,
    users, values, turned, slot_list, slot_count, diag, diag_in, work, part, in1, sum1, in2, total, upper_ref, below_ref,
    load_sem, store_sem, z_send, z_recv, core_send, core_recv, ds_send, ds_recv, dg_send, dg_recv, half_sem,
    s1_send, s1_recv, s2_send, s2_recv, s3_send, s3_recv, s4_send, s4_recv,
):
    user = lax.axis_index("user")
    item = lax.axis_index("item")
    y, x = user // SIDE, user % SIDE
    z, core = item // 2, item % 2
    other = 1 - core

    def at_xy(dy, dx):
        return ((y + dy) % SIDE) * SIDE + (x + dx) % SIDE

    z_ids = [(user, ((z + d) % DEPTH) * 2 + core) for d in FAR_FIRST_Z]
    xy_ids = [(at_xy(*d), item) for d in FAR_FIRST_XY]
    core_id = (user, z * 2 + other)

    def remote(src, dst, send, recv, device):
        return pltpu.make_async_remote_copy(
            src_ref=src, dst_ref=dst, send_sem=send, recv_sem=recv, device_id=device, device_id_type=MESH
        )

    def start(copies):
        for copy in copies:
            copy.start()

    def wait(copies):
        for copy in copies:
            copy.wait()

    barrier = pltpu.get_barrier_semaphore()
    for device in z_ids + xy_ids + [core_id]:
        pl.semaphore_signal(barrier, inc=1, device_id=device, device_id_type=MESH)

    own_load = pltpu.make_async_copy(panel_ref, users.at[core, z], load_sem.at[0])
    loads = [
        pltpu.make_async_copy(list_ref, slot_list, load_sem.at[1]),
        pltpu.make_async_copy(count_ref, slot_count, load_sem.at[2]),
    ] + [
        pltpu.make_async_copy(values_ref.at[:, :, c], values.at[c, pl.ds(0, BLK_DEV - 1)], load_sem.at[3 + c])
        for c in range(2)
    ]
    start([own_load] + loads)
    for c in range(2):
        values[c, BLK_DEV - 1] = jnp.zeros((DEPTH, SHARE, BLOCK), jnp.bfloat16)
    own_load.wait()
    pl.semaphore_wait(barrier, len(z_ids) + len(xy_ids) + 1)

    z_copies = [
        remote(users.at[core, z], users.at[core, z], z_send.at[k], z_recv.at[k], device)
        for k, device in enumerate(z_ids)
    ]
    start(z_copies)
    core_copies = []
    for k, d in enumerate((0,) + FAR_FIRST_Z):
        came_from = (z + DEPTH - d) % DEPTH
        core_copies.append(
            remote(users.at[core, came_from], users.at[core, came_from], core_send.at[k], core_recv.at[k], core_id)
        )
    core_copies[0].start()

    wait(loads)
    used = slot_count[0, 0]
    for b in range(BLK_DEV):
        slot = jnp.int32(BLK_DEV - 1)
        for k in range(BLK_DEV - 1):
            slot = jnp.where((slot_list[0, k] == b) & (k < used), k, slot)
        for c in range(2):
            block = values[c, slot].reshape(DEPTH * SHARE, BLOCK)
            turned[pl.ds(b * BLOCK, BLOCK), pl.ds(c * DEPTH * SHARE, DEPTH * SHARE)] = block.T

    for k in reversed(range(DEPTH - 1)):
        z_copies[k].wait_recv()
        core_copies[k + 1].start()
    wait(core_copies)
    for copy in z_copies:
        copy.wait_send()

    along = (
        [((at_xy(0, d), item), (x + d) % SIDE) for d in FAR_FIRST_SIDE],
        [((at_xy(d, 0), item), (y + d) % SIDE) for d in FAR_FIRST_SIDE],
    )
    place = (x, y)
    piece = ROWS // PIECES
    big, small = piece // SIDE, piece // SIDE**2

    def big_rows(q, i):
        return pl.ds(pl.multiple_of(q * piece + i * big, big), big)

    def small_rows(q, i):
        return pl.ds(pl.multiple_of(q * piece + i * small, small), small)

    def own_rows(q, h):
        return small_rows(q, place[h] * SIDE + place[1 - h])

    pairs = [(k, h) for k in range(SIDE - 1) for h in range(2)]
    s1 = [
        [
            remote(
                part.at[h, big_rows(q, along[h][k][1])], in1.at[q, h, k],
                s1_send.at[q, h, k], s1_recv.at[q, h, k], along[h][k][0],
            )
            for k, h in pairs
        ]
        for q in range(PIECES)
    ]
    s2 = [
        [
            remote(
                sum1.at[q, h, pl.ds(pl.multiple_of(along[1 - h][k][1] * small, small), small)], in2.at[q, h, k],
                s2_send.at[q, h, k], s2_recv.at[q, h, k], along[1 - h][k][0],
            )
            for k, h in pairs
        ]
        for q in range(PIECES)
    ]
    s3 = [
        [
            remote(
                total.at[h, own_rows(q, h)], total.at[h, own_rows(q, h)],
                s3_send.at[q, h, k], s3_recv.at[q, h, k], along[1 - h][k][0],
            )
            for k, h in pairs
        ]
        for q in range(PIECES)
    ]
    s4 = [
        [
            remote(
                total.at[h, big_rows(q, place[h])], total.at[h, big_rows(q, place[h])],
                s4_send.at[q, h, k], s4_recv.at[q, h, k], along[h][k][0],
            )
            for k, h in pairs
        ]
        for q in range(PIECES)
    ]

    gathered = users[...].reshape(2 * DEPTH * SHARE, PANEL)
    for q in range(PIECES):
        rows = pl.ds(q * piece, piece)
        below = jnp.dot(turned[rows, :], gathered, preferred_element_type=jnp.float32)
        for h in range(2):
            part[h, rows, :] = below[:, h * BLOCK : (h + 1) * BLOCK]
        start(s1[q])

    def diag_rows(device_user):
        return pl.ds(pl.multiple_of((core * SIDE * SIDE + device_user) * TILE, TILE), TILE)

    diag[...] = lax.dot_general(
        gathered, gathered, (((0,), (0,)), ((), ())), preferred_element_type=jnp.float32
    )
    ds_copies = [
        remote(diag.at[diag_rows(d[0])], diag_in.at[user], ds_send.at[k], ds_recv.at[k], d)
        for k, d in enumerate(xy_ids)
    ]
    start(ds_copies)
    diag_in[user] = diag[diag_rows(user), :]
    wait(ds_copies)
    diag_sum = diag_in[0]
    for k in range(1, SIDE * SIDE):
        diag_sum = diag_sum + diag_in[k]
    row = lax.broadcasted_iota(jnp.int32, (TILE, PANEL), 0) + (core * SIDE * SIDE + user) * TILE
    col = lax.broadcasted_iota(jnp.int32, (TILE, PANEL), 1)
    work[diag_rows(user), :] = diag_sum + jnp.where(row == col, 0.5, 0.0)
    dg_copies = [
        remote(work.at[diag_rows(user)], work.at[diag_rows(user)], dg_send.at[k], dg_recv.at[k], d)
        for k, d in enumerate(xy_ids)
    ]
    start(dg_copies)
    core_half = pl.ds(pl.multiple_of(core * BLOCK, BLOCK), BLOCK)
    half_copy = remote(work.at[core_half], work.at[core_half], half_sem.at[0], half_sem.at[1], core_id)

    for q in range(PIECES):
        wait(s1[q])
        for h in range(2):
            sum1[q, h] = part[h, big_rows(q, place[h]), :] + in1[q, h, 0] + in1[q, h, 1] + in1[q, h, 2]
        start(s2[q])

    for what, n in ORDER:
        if what == "diag":
            wait(dg_copies)
            half_copy.start()
            half_copy.wait()
        elif what == "factor":
            factor_step(n, work, upper_ref)
        elif what == "sum":
            wait(s2[n])
            for h in range(2):
                mine = sum1[n, h, pl.ds(pl.multiple_of(place[1 - h] * small, small), small), :]
                total[h, own_rows(n, h), :] = mine + in2[n, h, 0] + in2[n, h, 1] + in2[n, h, 2]
            start(s3[n])
        else:
            wait(s3[n])
            start(s4[n])
    upper_ref[...] = upper_ref[...].T
    stores = [pltpu.make_async_copy(upper_ref, diag_out, store_sem.at[PIECES])]
    start(stores)

    for q in range(PIECES):
        wait(s4[q])
        rows = pl.ds(q * piece, piece)
        below_ref[rows, :] = lax.dot_general(
            jnp.concatenate([total[0, rows, :], total[1, rows, :]], 1), work[...], (((1,), (1,)), ((), ())),
            precision=lax.Precision.HIGHEST, preferred_element_type=jnp.float32,
        )
        stores.append(pltpu.make_async_copy(below_ref.at[rows], below_out.at[rows], store_sem.at[q]))
        stores[-1].start()
    wait(stores)


def store_kernel(diag_ref, below_ref, diag_out, below_out):
    diag_out[...] = diag_ref[...]
    below_out[...] = below_ref[...]


def on_device(panel_users, block_values, block_list, block_count):
    f32, bf16 = jnp.float32, jnp.bfloat16
    slots = block_values.shape[1]
    values = block_values.transpose(1, 0, 2).reshape(slots, DEPTH, 2, SHARE, BLOCK)
    vmem = pl.BlockSpec(memory_space=pltpu.VMEM)
    hbm = pl.BlockSpec(memory_space=pltpu.HBM)
    sems = pltpu.SemaphoreType.DMA
    xy = SIDE * SIDE - 1
    big, small = ROWS // PIECES // SIDE, ROWS // PIECES // SIDE**2
    out_shape = [jax.ShapeDtypeStruct((PANEL, PANEL), f32), jax.ShapeDtypeStruct((ROWS, PANEL), f32)]
    diag, below = pl.pallas_call(
        gram_kernel,
        out_shape=out_shape,
        in_specs=[hbm, hbm, hbm, hbm],
        out_specs=[hbm, hbm],
        scratch_shapes=[
            pltpu.VMEM((2, DEPTH, SHARE, PANEL), bf16),
            pltpu.VMEM((2, BLK_DEV, DEPTH, SHARE, BLOCK), bf16),
            pltpu.VMEM((ROWS, 2 * DEPTH * SHARE), bf16),
            pltpu.SMEM((1, slots), jnp.int32),
            pltpu.SMEM((1, 1), jnp.int32),
            pltpu.VMEM((PANEL, PANEL), f32),
            pltpu.VMEM((SIDE * SIDE, TILE, PANEL), f32),
            pltpu.VMEM((PANEL, PANEL), f32),
            pltpu.VMEM((2, ROWS, BLOCK), f32),
            pltpu.VMEM((PIECES, 2, SIDE - 1, big, BLOCK), f32),
            pltpu.VMEM((PIECES, 2, big, BLOCK), f32),
            pltpu.VMEM((PIECES, 2, SIDE - 1, small, BLOCK), f32),
            pltpu.VMEM((2, ROWS, BLOCK), f32),
            pltpu.VMEM((PANEL, PANEL), f32),
            pltpu.VMEM((ROWS, PANEL), f32),
            sems((5,)),
            sems((PIECES + 1,)),
            sems((DEPTH - 1,)),
            sems((DEPTH - 1,)),
            sems((DEPTH,)),
            sems((DEPTH,)),
            sems((xy,)),
            sems((xy,)),
            sems((xy,)),
            sems((xy,)),
            sems((2,)),
        ]
        + [sems((PIECES, 2, SIDE - 1))] * 8,
        compiler_params=pltpu.CompilerParams(
            collective_id=0, has_side_effects=True, vmem_limit_bytes=56 << 20
        ),
        name="gram",
    )(panel_users, values, block_list, block_count)
    whole = pl.BlockSpec((PANEL, PANEL), lambda i: (0, 0))
    rows = pl.BlockSpec((ROWS // STORES, PANEL), lambda i: (i, 0))
    return pl.pallas_call(
        store_kernel,
        grid=(STORES,),
        out_shape=out_shape,
        in_specs=[whole, rows],
        out_specs=[whole, rows],
        compiler_params=pltpu.CompilerParams(vmem_limit_bytes=56 << 20),
        name="store",
    )(diag, below)


def solution(mesh):
    in_specs = (
        P(("user", "item"), None),
        P("user", "item", None),
        P("user", "item"),
        P("user", "item"),
    )
    out_specs = (P(), P("item", None))
    return jax.shard_map(
        on_device, mesh=mesh, in_specs=in_specs, out_specs=out_specs, check_vma=False
    )
```

```python
import jax
import jax.numpy as jnp
from jax import lax
from jax.sharding import PartitionSpec as P
import jax.experimental.pallas as pl
import jax.experimental.pallas.tpu as pltpu

BLOCK = 128
PANEL = 256
BLK_DEV = 8
ROWS = BLK_DEV * BLOCK
SIDE = 4
DEPTH = 16
SHARE = 16
TILE = 8
NB = 32
STORES = 4
PIECES = 4
MESH = pl.DeviceIdType.MESH
FAR_FIRST_Z = (8, 7, 9, 6, 10, 5, 11, 4, 12, 3, 13, 2, 14, 1, 15)
FAR_FIRST_XY = sorted(
    ((dy, dx) for dy in range(SIDE) for dx in range(SIDE) if dy or dx),
    key=lambda d: -(min(d[0], SIDE - d[0]) + min(d[1], SIDE - d[1])),
)
FAR_FIRST_SIDE = (2, 1, 3)
ORDER = (
    ("sum", 0), ("sum", 1), ("half", 0), ("sum", 2), ("diag", 0), ("factor", 0), ("sum", 3), ("pass", 0), ("factor", 1),
    ("pass", 1), ("factor", 2), ("pass", 2), ("factor", 3), ("pass", 3), ("factor", 4), ("factor", 5), ("factor", 6),
    ("factor", 7),
)


def split3(x):
    high = x.astype(jnp.bfloat16)
    rest = x - high.astype(jnp.float32)
    middle = rest.astype(jnp.bfloat16)
    low = (rest - middle.astype(jnp.float32)).astype(jnp.bfloat16)
    return high, middle, low


def eliminate(rows, inverse, start, count):
    left = rows.shape[0]
    columns = jnp.stack([jnp.broadcast_to(rows[:, start + t : start + t + 1], (left, BLOCK)) for t in range(count)])
    tile_sub = lax.broadcasted_iota(jnp.int32, (8, BLOCK), 0)
    rows_done, inverse_done, pivots = [], [], None
    for t in range(count):
        s = t % 8
        here = columns[0]
        pivots = jnp.where(tile_sub == s, here[:8], pivots) if s else here[:8]
        reciprocal = 1.0 / here[s : s + 1]
        below = jnp.where(lax.broadcasted_iota(jnp.int32, (left, BLOCK), 0) > s, here, 0.0)
        if t < count - 1:
            columns = columns[1:] - (below[None] * columns[1:, s : s + 1]) * reciprocal[None]
        scaled = below * reciprocal
        rows = rows - jnp.concatenate([scaled, scaled], 1) * rows[s : s + 1]
        inverse = inverse - scaled * inverse[s : s + 1]
        if s == 7:
            scale = lax.rsqrt(pivots)
            rows_done.append(rows[:8] * jnp.concatenate([scale, scale], 1))
            inverse_done.append(inverse[:8] * scale)
            left -= 8
            if left:
                rows, inverse, columns = rows[8:], inverse[8:], columns[:, 8:]
    return rows_done, inverse_done, rows, inverse


def factor_step(step, work_ref, upper_ref):
    start, stop = NB * step, NB * (step + 1)
    rows = work_ref[start:stop, :]
    lane = lax.broadcasted_iota(jnp.int32, (NB, BLOCK), 1)
    sub = lax.broadcasted_iota(jnp.int32, (NB, BLOCK), 0)
    inverse = jnp.where(lane == sub + start % BLOCK, 1.0, 0.0).astype(jnp.float32)
    rows1, inverse1, rows, inverse = eliminate(rows, inverse, start, NB // 2)
    rows2, inverse2, _, _ = eliminate(rows, inverse, start + NB // 2, NB // 2)
    upper = jnp.concatenate(rows1 + rows2, 0)
    inverse = jnp.concatenate(inverse1 + inverse2, 0)
    col = lax.broadcasted_iota(jnp.int32, (NB, PANEL), 1)
    row = lax.broadcasted_iota(jnp.int32, (NB, PANEL), 0)
    done = jnp.where((col >= start) & (col < stop), jnp.concatenate([inverse, inverse], 1), upper)
    upper_ref[start:stop, :] = jnp.where(col >= row + start, upper, 0.0)
    work_ref[start:stop, :] = jnp.where(col < stop, done, 0.0)
    if stop == PANEL:
        return
    base = BLOCK * (stop // BLOCK)
    dh, dm, dl = split3(done)
    ih, im, il = split3(upper[:, base:])
    product = lax.dot_general(
        jnp.concatenate([ih, ih, im, ih, im, il], 0),
        jnp.concatenate([dh, dm, dh, dl, dm, dh], 0),
        (((0,), (0,)), ((), ())),
        preferred_element_type=jnp.float32,
    )
    wide = lax.broadcasted_iota(jnp.int32, (PANEL - stop, PANEL), 1)
    kept = jnp.where((wide >= start) & (wide < stop), 0.0, work_ref[stop:, :])
    work_ref[stop:, :] = kept - product[stop - base :, :]


def gram_kernel(
    panel_ref, values_ref, list_ref, count_ref, upper_ref, work, total,
    users, values, turned, slot_list, diag, diag_in, part, in1, sum1, in2,
    load_sem, z_send, z_recv, core_send, core_recv, ds_send, ds_recv, dg_send, dg_recv, half_sem,
    s1_send, s1_recv, s2_send, s2_recv, s3_send, s3_recv, s4_send, s4_recv,
):
    user = lax.axis_index("user")
    item = lax.axis_index("item")
    y, x = user // SIDE, user % SIDE
    z, core = item // 2, item % 2
    other = 1 - core

    def at_xy(dy, dx):
        return ((y + dy) % SIDE) * SIDE + (x + dx) % SIDE

    z_ids = [(user, ((z + d) % DEPTH) * 2 + core) for d in FAR_FIRST_Z]
    xy_ids = [(at_xy(*d), item) for d in FAR_FIRST_XY]
    core_id = (user, z * 2 + other)

    def remote(src, dst, send, recv, device):
        return pltpu.make_async_remote_copy(
            src_ref=src, dst_ref=dst, send_sem=send, recv_sem=recv, device_id=device, device_id_type=MESH
        )

    def start(copies):
        for copy in copies:
            copy.start()

    def wait(copies):
        for copy in copies:
            copy.wait()

    barrier = pltpu.get_barrier_semaphore()
    for device in z_ids + xy_ids + [core_id]:
        pl.semaphore_signal(barrier, inc=1, device_id=device, device_id_type=MESH)

    own_load = pltpu.make_async_copy(panel_ref, users.at[core, z], load_sem.at[0])
    loads = [pltpu.make_async_copy(list_ref, slot_list, load_sem.at[1])] + [
        pltpu.make_async_copy(values_ref.at[:, :, c], values.at[c, pl.ds(0, BLK_DEV - 1)], load_sem.at[2 + c])
        for c in range(2)
    ]
    start([own_load] + loads)
    for c in range(2):
        values[c, BLK_DEV - 1] = jnp.zeros((DEPTH, SHARE, BLOCK), jnp.bfloat16)
    own_load.wait()
    pl.semaphore_wait(barrier, len(z_ids) + len(xy_ids) + 1)

    z_copies = [
        remote(users.at[core, z], users.at[core, z], z_send.at[k], z_recv.at[k], device)
        for k, device in enumerate(z_ids)
    ]
    start(z_copies)
    core_copies = []
    for k, d in enumerate((0,) + FAR_FIRST_Z):
        came_from = (z + DEPTH - d) % DEPTH
        core_copies.append(
            remote(users.at[core, came_from], users.at[core, came_from], core_send.at[k], core_recv.at[k], core_id)
        )
    core_copies[0].start()

    wait(loads)
    used = count_ref[0, 0]
    for b in range(BLK_DEV):
        slot = jnp.int32(BLK_DEV - 1)
        for k in range(BLK_DEV - 1):
            slot = jnp.where((slot_list[0, k] == b) & (k < used), k, slot)
        for c in range(2):
            block = values[c, slot].reshape(DEPTH * SHARE, BLOCK)
            turned[pl.ds(b * BLOCK, BLOCK), pl.ds(c * DEPTH * SHARE, DEPTH * SHARE)] = block.T

    for k in reversed(range(DEPTH - 1)):
        z_copies[k].wait_recv()
        core_copies[k + 1].start()
    wait(core_copies)
    for copy in z_copies:
        copy.wait_send()

    along = (
        [((at_xy(0, d), item), (x + d) % SIDE) for d in FAR_FIRST_SIDE],
        [((at_xy(d, 0), item), (y + d) % SIDE) for d in FAR_FIRST_SIDE],
    )
    place = (x, y)
    piece = ROWS // PIECES
    big, small = piece // SIDE, piece // SIDE**2

    def big_rows(q, i):
        return pl.ds(pl.multiple_of(q * piece + i * big, big), big)

    def small_rows(q, i):
        return pl.ds(pl.multiple_of(q * piece + i * small, small), small)

    def own_rows(q, h):
        return small_rows(q, place[h] * SIDE + place[1 - h])

    pairs = [(k, h) for k in range(SIDE - 1) for h in range(2)]
    s1 = [
        [
            remote(
                part.at[h, big_rows(q, along[h][k][1])], in1.at[q, h, k],
                s1_send.at[q, h, k], s1_recv.at[q, h, k], along[h][k][0],
            )
            for k, h in pairs
        ]
        for q in range(PIECES)
    ]
    s2 = [
        [
            remote(
                sum1.at[q, h, pl.ds(pl.multiple_of(along[1 - h][k][1] * small, small), small)], in2.at[q, h, k],
                s2_send.at[q, h, k], s2_recv.at[q, h, k], along[1 - h][k][0],
            )
            for k, h in pairs
        ]
        for q in range(PIECES)
    ]
    s3 = [
        [
            remote(
                total.at[h, own_rows(q, h)], total.at[h, own_rows(q, h)],
                s3_send.at[q, h, k], s3_recv.at[q, h, k], along[1 - h][k][0],
            )
            for k, h in pairs
        ]
        for q in range(PIECES)
    ]
    s4 = [
        [
            remote(
                total.at[h, big_rows(q, place[h])], total.at[h, big_rows(q, place[h])],
                s4_send.at[q, h, k], s4_recv.at[q, h, k], along[h][k][0],
            )
            for k, h in pairs
        ]
        for q in range(PIECES)
    ]

    gathered = users[...].reshape(2 * DEPTH * SHARE, PANEL)
    def diag_rows(device_user):
        return pl.ds(pl.multiple_of((core * SIDE * SIDE + device_user) * TILE, TILE), TILE)

    diag[...] = lax.dot_general(
        gathered, gathered, (((0,), (0,)), ((), ())), preferred_element_type=jnp.float32
    )
    ds_copies = [
        remote(diag.at[diag_rows(d[0])], diag_in.at[user], ds_send.at[k], ds_recv.at[k], d)
        for k, d in enumerate(xy_ids)
    ]
    start(ds_copies)
    diag_in[user] = diag[diag_rows(user), :]
    for q in range(PIECES):
        rows = pl.ds(q * piece, piece)
        below = jnp.dot(turned[rows, :], gathered, preferred_element_type=jnp.float32)
        for h in range(2):
            part[h, rows, :] = below[:, h * BLOCK : (h + 1) * BLOCK]
        start(s1[q])

    wait(ds_copies)
    diag_sum = diag_in[0]
    for k in range(1, SIDE * SIDE):
        diag_sum = diag_sum + diag_in[k]
    row = lax.broadcasted_iota(jnp.int32, (TILE, PANEL), 0) + (core * SIDE * SIDE + user) * TILE
    col = lax.broadcasted_iota(jnp.int32, (TILE, PANEL), 1)
    work[diag_rows(user), :] = diag_sum + jnp.where(row == col, 0.5, 0.0)
    dg_copies = [
        remote(work.at[diag_rows(user)], work.at[diag_rows(user)], dg_send.at[k], dg_recv.at[k], d)
        for k, d in enumerate(xy_ids)
    ]
    start(dg_copies)
    core_half = pl.ds(pl.multiple_of(core * BLOCK, BLOCK), BLOCK)
    half_copy = remote(work.at[core_half], work.at[core_half], half_sem.at[0], half_sem.at[1], core_id)

    for q in range(PIECES):
        wait(s1[q])
        for h in range(2):
            sum1[q, h] = part[h, big_rows(q, place[h]), :] + in1[q, h, 0] + in1[q, h, 1] + in1[q, h, 2]
        start(s2[q])

    for what, n in ORDER:
        if what == "half":
            wait(dg_copies)
            half_copy.start()
        elif what == "diag":
            half_copy.wait()
        elif what == "factor":
            factor_step(n, work, upper_ref)
        elif what == "sum":
            wait(s2[n])
            for h in range(2):
                mine = sum1[n, h, pl.ds(pl.multiple_of(place[1 - h] * small, small), small), :]
                total[h, own_rows(n, h), :] = mine + in2[n, h, 0] + in2[n, h, 1] + in2[n, h, 2]
            start(s3[n])
        else:
            wait(s3[n])
            start(s4[n])
    for q in range(PIECES):
        wait(s4[q])


def solve_kernel(upper_ref, inverse_ref, total_ref, diag_out, below_out, lower, below, sem):
    stores = []
    for i in range(STORES):
        rows = pl.ds(i * (ROWS // STORES), ROWS // STORES)
        below[rows, :] = lax.dot_general(
            jnp.concatenate([total_ref[0, rows, :], total_ref[1, rows, :]], 1), inverse_ref[...],
            (((1,), (1,)), ((), ())),
            precision=lax.Precision.HIGHEST, preferred_element_type=jnp.float32,
        )
        stores.append(pltpu.make_async_copy(below.at[rows], below_out.at[rows], sem.at[i]))
        stores[-1].start()
    lower[...] = upper_ref[...].T
    stores.append(pltpu.make_async_copy(lower, diag_out, sem.at[STORES]))
    stores[-1].start()
    for store in stores:
        store.wait()


def on_device(panel_users, block_values, block_list, block_count):
    f32, bf16 = jnp.float32, jnp.bfloat16
    slots = block_values.shape[1]
    values = block_values.transpose(1, 0, 2).reshape(slots, DEPTH, 2, SHARE, BLOCK)
    vmem = pl.BlockSpec(memory_space=pltpu.VMEM)
    hbm = pl.BlockSpec(memory_space=pltpu.HBM)
    sems = pltpu.SemaphoreType.DMA
    xy = SIDE * SIDE - 1
    big, small = ROWS // PIECES // SIDE, ROWS // PIECES // SIDE**2
    upper, inverse, total = pl.pallas_call(
        gram_kernel,
        out_shape=[
            pltpu.VMEM((PANEL, PANEL), f32),
            pltpu.VMEM((PANEL, PANEL), f32),
            pltpu.VMEM((2, ROWS, BLOCK), f32),
        ],
        in_specs=[hbm, hbm, hbm, pl.BlockSpec(memory_space=pltpu.SMEM)],
        out_specs=[vmem, vmem, vmem],
        scratch_shapes=[
            pltpu.VMEM((2, DEPTH, SHARE, PANEL), bf16),
            pltpu.VMEM((2, BLK_DEV, DEPTH, SHARE, BLOCK), bf16),
            pltpu.VMEM((ROWS, 2 * DEPTH * SHARE), bf16),
            pltpu.SMEM((1, slots), jnp.int32),
            pltpu.VMEM((PANEL, PANEL), f32),
            pltpu.VMEM((SIDE * SIDE, TILE, PANEL), f32),
            pltpu.VMEM((2, ROWS, BLOCK), f32),
            pltpu.VMEM((PIECES, 2, SIDE - 1, big, BLOCK), f32),
            pltpu.VMEM((PIECES, 2, big, BLOCK), f32),
            pltpu.VMEM((PIECES, 2, SIDE - 1, small, BLOCK), f32),
            sems((4,)),
            sems((DEPTH - 1,)),
            sems((DEPTH - 1,)),
            sems((DEPTH,)),
            sems((DEPTH,)),
            sems((xy,)),
            sems((xy,)),
            sems((xy,)),
            sems((xy,)),
            sems((2,)),
        ]
        + [sems((PIECES, 2, SIDE - 1))] * 8,
        compiler_params=pltpu.CompilerParams(
            collective_id=0, has_side_effects=True, vmem_limit_bytes=32 << 20
        ),
        name="gram",
    )(*[pltpu.with_memory_space_constraint(a, pltpu.HBM) for a in (panel_users, values, block_list)], block_count)
    return pl.pallas_call(
        solve_kernel,
        out_shape=[jax.ShapeDtypeStruct((PANEL, PANEL), f32), jax.ShapeDtypeStruct((ROWS, PANEL), f32)],
        in_specs=[vmem] * 3,
        out_specs=[hbm] * 2,
        scratch_shapes=[pltpu.VMEM((PANEL, PANEL), f32), pltpu.VMEM((ROWS, PANEL), f32), sems((STORES + 1,))],
        compiler_params=pltpu.CompilerParams(vmem_limit_bytes=16 << 20),
        name="solve",
    )(upper, inverse, total)


def solution(mesh):
    in_specs = (
        P(("user", "item"), None),
        P("user", "item", None),
        P("user", "item"),
        P("user", "item"),
    )
    out_specs = (P(), P("item", None))
    return jax.shard_map(
        on_device, mesh=mesh, in_specs=in_specs, out_specs=out_specs, check_vma=False
    )
```

```python
import jax
import jax.numpy as jnp
from jax import lax
from jax.sharding import PartitionSpec as P
import jax.experimental.pallas as pl
import jax.experimental.pallas.tpu as pltpu

BLOCK = 128
PANEL = 256
BLK_DEV = 8
ROWS = BLK_DEV * BLOCK
SIDE = 4
DEPTH = 16
SHARE = 16
TILE = 8
NB = 32
STORES = 4
PIECES = 4
MESH = pl.DeviceIdType.MESH
REACH = 4
NEAR_Z = (4, -4, 3, -3, 2, -2, 1, -1)
FAR_FIRST_XY = sorted(
    ((dy, dx) for dy in range(SIDE) for dx in range(SIDE) if dy or dx),
    key=lambda d: -(min(d[0], SIDE - d[0]) + min(d[1], SIDE - d[1])),
)
FAR_FIRST_SIDE = (2, 1, 3)
ORDER = (
    ("sum", 0), ("sum", 1), ("half", 0), ("sum", 2), ("diag", 0), ("factor", 0), ("sum", 3), ("pass", 0), ("factor", 1),
    ("pass", 1), ("factor", 2), ("pass", 2), ("factor", 3), ("pass", 3), ("factor", 4), ("factor", 5), ("factor", 6),
    ("factor", 7),
)


def split3(x):
    high = x.astype(jnp.bfloat16)
    rest = x - high.astype(jnp.float32)
    middle = rest.astype(jnp.bfloat16)
    low = (rest - middle.astype(jnp.float32)).astype(jnp.bfloat16)
    return high, middle, low


def eliminate(rows, inverse, start, count):
    left = rows.shape[0]
    columns = jnp.stack([jnp.broadcast_to(rows[:, start + t : start + t + 1], (left, BLOCK)) for t in range(count)])
    tile_sub = lax.broadcasted_iota(jnp.int32, (8, BLOCK), 0)
    rows_done, inverse_done, pivots = [], [], None
    for t in range(count):
        s = t % 8
        here = columns[0]
        pivots = jnp.where(tile_sub == s, here[:8], pivots) if s else here[:8]
        reciprocal = 1.0 / here[s : s + 1]
        below = jnp.where(lax.broadcasted_iota(jnp.int32, (left, BLOCK), 0) > s, here, 0.0)
        if t < count - 1:
            columns = columns[1:] - (below[None] * columns[1:, s : s + 1]) * reciprocal[None]
        scaled = below * reciprocal
        rows = rows - jnp.concatenate([scaled, scaled], 1) * rows[s : s + 1]
        inverse = inverse - scaled * inverse[s : s + 1]
        if s == 7:
            scale = lax.rsqrt(pivots)
            rows_done.append(rows[:8] * jnp.concatenate([scale, scale], 1))
            inverse_done.append(inverse[:8] * scale)
            left -= 8
            if left:
                rows, inverse, columns = rows[8:], inverse[8:], columns[:, 8:]
    return rows_done, inverse_done, rows, inverse


def factor_step(step, work_ref, upper_ref):
    start, stop = NB * step, NB * (step + 1)
    rows = work_ref[start:stop, :]
    lane = lax.broadcasted_iota(jnp.int32, (NB, BLOCK), 1)
    sub = lax.broadcasted_iota(jnp.int32, (NB, BLOCK), 0)
    inverse = jnp.where(lane == sub + start % BLOCK, 1.0, 0.0).astype(jnp.float32)
    rows1, inverse1, rows, inverse = eliminate(rows, inverse, start, NB // 2)
    rows2, inverse2, _, _ = eliminate(rows, inverse, start + NB // 2, NB // 2)
    upper = jnp.concatenate(rows1 + rows2, 0)
    inverse = jnp.concatenate(inverse1 + inverse2, 0)
    col = lax.broadcasted_iota(jnp.int32, (NB, PANEL), 1)
    row = lax.broadcasted_iota(jnp.int32, (NB, PANEL), 0)
    done = jnp.where((col >= start) & (col < stop), jnp.concatenate([inverse, inverse], 1), upper)
    upper_ref[start:stop, :] = jnp.where(col >= row + start, upper, 0.0)
    work_ref[start:stop, :] = jnp.where(col < stop, done, 0.0)
    if stop == PANEL:
        return
    base = BLOCK * (stop // BLOCK)
    dh, dm, dl = split3(done)
    ih, im, il = split3(upper[:, base:])
    product = lax.dot_general(
        jnp.concatenate([ih, ih, im, ih, im, il], 0),
        jnp.concatenate([dh, dm, dh, dl, dm, dh], 0),
        (((0,), (0,)), ((), ())),
        preferred_element_type=jnp.float32,
    )
    wide = lax.broadcasted_iota(jnp.int32, (PANEL - stop, PANEL), 1)
    kept = jnp.where((wide >= start) & (wide < stop), 0.0, work_ref[stop:, :])
    work_ref[stop:, :] = kept - product[stop - base :, :]


def gram_kernel(
    panel_ref, values_ref, list_ref, count_ref, upper_ref, work, total,
    users, values, turned, slot_list, diag, diag_in, part, in1, sum1, in2,
    load_sem, z_send, z_recv, f_send, f_recv, core_send, core_recv, ds_send, ds_recv, dg_send, dg_recv, half_sem,
    s1_send, s1_recv, s2_send, s2_recv, s3_send, s3_recv, s4_send, s4_recv,
):
    user = lax.axis_index("user")
    item = lax.axis_index("item")
    y, x = user // SIDE, user % SIDE
    z, core = item // 2, item % 2
    other = 1 - core

    def at_xy(dy, dx):
        return ((y + dy) % SIDE) * SIDE + (x + dx) % SIDE

    def at_z(d):
        return (z + DEPTH + d) % DEPTH

    z_ids = [(user, at_z(d) * 2 + core) for d in NEAR_Z]
    xy_ids = [(at_xy(*d), item) for d in FAR_FIRST_XY]
    core_id = (user, z * 2 + other)

    def remote(src, dst, send, recv, device):
        return pltpu.make_async_remote_copy(
            src_ref=src, dst_ref=dst, send_sem=send, recv_sem=recv, device_id=device, device_id_type=MESH
        )

    def start(copies):
        for copy in copies:
            copy.start()

    def wait(ref, sem):
        pltpu.make_async_copy(ref, ref, sem).wait()

    barrier = pltpu.get_barrier_semaphore()
    for device in z_ids + xy_ids + [core_id]:
        pl.semaphore_signal(barrier, inc=1, device_id=device, device_id_type=MESH)

    own_load = pltpu.make_async_copy(panel_ref, users.at[core, z], load_sem.at[0])
    loads = [pltpu.make_async_copy(list_ref, slot_list, load_sem.at[1])] + [
        pltpu.make_async_copy(values_ref.at[:, :, c], values.at[c, pl.ds(0, BLK_DEV - 1)], load_sem.at[2 + c])
        for c in range(2)
    ]
    start([own_load] + loads)
    for c in range(2):
        values[c, BLK_DEV - 1] = jnp.zeros((DEPTH, SHARE, BLOCK), jnp.bfloat16)
    own_load.wait()
    pl.semaphore_wait(barrier, len(z_ids) + len(xy_ids) + 1)

    z_copies = [
        remote(users.at[core, z], users.at[core, z], z_send, z_recv.at[k], device)
        for k, device in enumerate(z_ids)
    ]
    start(z_copies)

    def pass_to_core(place):
        return remote(users.at[core, place], users.at[core, place], core_send, core_recv, core_id)

    pass_to_core(z).start()

    for load in loads:
        load.wait()
    used = count_ref[0, 0]
    for b in range(BLK_DEV):
        slot = jnp.int32(BLK_DEV - 1)
        for k in range(BLK_DEV - 1):
            slot = jnp.where((slot_list[0, k] == b) & (k < used), k, slot)
        for c in range(2):
            block = values[c, slot].reshape(DEPTH * SHARE, BLOCK)
            turned[pl.ds(b * BLOCK, BLOCK), pl.ds(c * DEPTH * SHARE, DEPTH * SHARE)] = block.T

    passed = []
    for k, d in reversed(list(enumerate(NEAR_Z))):
        z_copies[k].wait_recv()
        came_from = at_z(-d)
        if d != -REACH:
            ahead = (user, at_z(REACH if d > 0 else -REACH) * 2 + core)
            f = len(passed)
            copy = remote(users.at[core, came_from], users.at[core, came_from], f_send, f_recv.at[f], ahead)
            copy.start()
            passed.append((copy, at_z(-d - (REACH if d > 0 else -REACH))))
        pass_to_core(came_from).start()
    for copy, came_from in passed:
        copy.wait_recv()
        pass_to_core(came_from).start()
    wait(users.at[other], core_recv)
    wait(users.at[core], core_send)
    wait(users.at[core, pl.ds(0, len(z_copies))], z_send)
    wait(users.at[core, pl.ds(0, len(passed))], f_send)

    along = (
        [((at_xy(0, d), item), (x + d) % SIDE) for d in FAR_FIRST_SIDE],
        [((at_xy(d, 0), item), (y + d) % SIDE) for d in FAR_FIRST_SIDE],
    )
    place = (x, y)
    piece = ROWS // PIECES
    big, small = piece // SIDE, piece // SIDE**2

    def big_rows(q, i):
        return pl.ds(pl.multiple_of(q * piece + i * big, big), big)

    def small_rows(q, i):
        return pl.ds(pl.multiple_of(q * piece + i * small, small), small)

    def own_rows(q, h):
        return small_rows(q, place[h] * SIDE + place[1 - h])

    pairs = [(k, h) for k in range(SIDE - 1) for h in range(2)]
    s1 = [
        [
            remote(
                part.at[h, big_rows(q, along[h][k][1])], in1.at[q, h, k],
                s1_send, s1_recv.at[q], along[h][k][0],
            )
            for k, h in pairs
        ]
        for q in range(PIECES)
    ]
    s2 = [
        [
            remote(
                sum1.at[q, h, pl.ds(pl.multiple_of(along[1 - h][k][1] * small, small), small)], in2.at[q, h, k],
                s2_send, s2_recv.at[q], along[1 - h][k][0],
            )
            for k, h in pairs
        ]
        for q in range(PIECES)
    ]
    s3 = [
        [
            remote(
                total.at[h, own_rows(q, h)], total.at[h, own_rows(q, h)],
                s3_send, s3_recv.at[q], along[1 - h][k][0],
            )
            for k, h in pairs
        ]
        for q in range(PIECES)
    ]
    s4 = [
        [
            remote(
                total.at[h, big_rows(q, place[h])], total.at[h, big_rows(q, place[h])],
                s4_send, s4_recv.at[q], along[h][k][0],
            )
            for k, h in pairs
        ]
        for q in range(PIECES)
    ]

    gathered = users[...].reshape(2 * DEPTH * SHARE, PANEL)
    def diag_rows(device_user):
        return pl.ds(pl.multiple_of((core * SIDE * SIDE + device_user) * TILE, TILE), TILE)

    diag[...] = lax.dot_general(
        gathered, gathered, (((0,), (0,)), ((), ())), preferred_element_type=jnp.float32
    )
    ds_copies = [
        remote(diag.at[diag_rows(d[0])], diag_in.at[user], ds_send, ds_recv, d)
        for d in xy_ids
    ]
    start(ds_copies)
    diag_in[user] = diag[diag_rows(user), :]
    for q in range(PIECES):
        rows = pl.ds(q * piece, piece)
        below = jnp.dot(turned[rows, :], gathered, preferred_element_type=jnp.float32)
        for h in range(2):
            part[h, rows, :] = below[:, h * BLOCK : (h + 1) * BLOCK]
        start(s1[q])

    others = diag_in.at[pl.ds(0, len(xy_ids))]
    wait(others, ds_recv)
    diag_sum = diag_in[0]
    for k in range(1, SIDE * SIDE):
        diag_sum = diag_sum + diag_in[k]
    row = lax.broadcasted_iota(jnp.int32, (TILE, PANEL), 0) + (core * SIDE * SIDE + user) * TILE
    col = lax.broadcasted_iota(jnp.int32, (TILE, PANEL), 1)
    work[diag_rows(user), :] = diag_sum + jnp.where(row == col, 0.5, 0.0)
    dg_copies = [
        remote(work.at[diag_rows(user)], work.at[diag_rows(user)], dg_send, dg_recv, d)
        for d in xy_ids
    ]
    start(dg_copies)
    core_half = pl.ds(pl.multiple_of(core * BLOCK, BLOCK), BLOCK)
    half_copy = remote(work.at[core_half], work.at[core_half], half_sem.at[0], half_sem.at[1], core_id)

    for q in range(PIECES):
        wait(in1.at[q], s1_recv.at[q])
        for h in range(2):
            sum1[q, h] = part[h, big_rows(q, place[h]), :] + in1[q, h, 0] + in1[q, h, 1] + in1[q, h, 2]
        start(s2[q])

    for what, n in ORDER:
        if what == "half":
            wait(others, dg_recv)
            wait(others, dg_send)
            half_copy.start()
        elif what == "diag":
            half_copy.wait()
        elif what == "factor":
            factor_step(n, work, upper_ref)
        elif what == "sum":
            wait(in2.at[n], s2_recv.at[n])
            for h in range(2):
                mine = sum1[n, h, pl.ds(pl.multiple_of(place[1 - h] * small, small), small), :]
                total[h, own_rows(n, h), :] = mine + in2[n, h, 0] + in2[n, h, 1] + in2[n, h, 2]
            start(s3[n])
        else:
            wait(in2.at[n], s3_recv.at[n])
            start(s4[n])
    for q in range(PIECES):
        wait(in1.at[q], s4_recv.at[q])
    wait(in1, s1_send)
    wait(in2, s2_send)
    wait(in2, s3_send)
    wait(in1, s4_send)
    wait(others, ds_send)


def solve_kernel(upper_ref, inverse_ref, total_ref, diag_out, below_out, lower, below, sem):
    stores = []
    for i in range(STORES):
        rows = pl.ds(i * (ROWS // STORES), ROWS // STORES)
        below[rows, :] = lax.dot_general(
            jnp.concatenate([total_ref[0, rows, :], total_ref[1, rows, :]], 1), inverse_ref[...],
            (((1,), (1,)), ((), ())),
            precision=lax.Precision.HIGHEST, preferred_element_type=jnp.float32,
        )
        stores.append(pltpu.make_async_copy(below.at[rows], below_out.at[rows], sem.at[i]))
        stores[-1].start()
    lower[...] = upper_ref[...].T
    stores.append(pltpu.make_async_copy(lower, diag_out, sem.at[STORES]))
    stores[-1].start()
    for store in stores:
        store.wait()


def on_device(panel_users, block_values, block_list, block_count):
    f32, bf16 = jnp.float32, jnp.bfloat16
    slots = block_values.shape[1]
    values = block_values.transpose(1, 0, 2).reshape(slots, DEPTH, 2, SHARE, BLOCK)
    vmem = pl.BlockSpec(memory_space=pltpu.VMEM)
    hbm = pl.BlockSpec(memory_space=pltpu.HBM)
    sems = pltpu.SemaphoreType.DMA
    big, small = ROWS // PIECES // SIDE, ROWS // PIECES // SIDE**2
    upper, inverse, total = pl.pallas_call(
        gram_kernel,
        out_shape=[
            pltpu.VMEM((PANEL, PANEL), f32),
            pltpu.VMEM((PANEL, PANEL), f32),
            pltpu.VMEM((2, ROWS, BLOCK), f32),
        ],
        in_specs=[hbm, hbm, hbm, pl.BlockSpec(memory_space=pltpu.SMEM)],
        out_specs=[vmem, vmem, vmem],
        scratch_shapes=[
            pltpu.VMEM((2, DEPTH, SHARE, PANEL), bf16),
            pltpu.VMEM((2, BLK_DEV, DEPTH, SHARE, BLOCK), bf16),
            pltpu.VMEM((ROWS, 2 * DEPTH * SHARE), bf16),
            pltpu.SMEM((1, slots), jnp.int32),
            pltpu.VMEM((PANEL, PANEL), f32),
            pltpu.VMEM((SIDE * SIDE, TILE, PANEL), f32),
            pltpu.VMEM((2, ROWS, BLOCK), f32),
            pltpu.VMEM((PIECES, 2, SIDE - 1, big, BLOCK), f32),
            pltpu.VMEM((PIECES, 2, big, BLOCK), f32),
            pltpu.VMEM((PIECES, 2, SIDE - 1, small, BLOCK), f32),
            sems((4,)),
            sems,
            sems((2 * REACH,)),
            sems,
            sems((2 * REACH - 1,)),
        ]
        + [sems] * 6
        + [sems((2,))]
        + [sems, sems((PIECES,))] * 4,
        compiler_params=pltpu.CompilerParams(
            collective_id=0, has_side_effects=True, vmem_limit_bytes=32 << 20
        ),
        name="gram",
    )(*[pltpu.with_memory_space_constraint(a, pltpu.HBM) for a in (panel_users, values, block_list)], block_count)
    return pl.pallas_call(
        solve_kernel,
        out_shape=[jax.ShapeDtypeStruct((PANEL, PANEL), f32), jax.ShapeDtypeStruct((ROWS, PANEL), f32)],
        in_specs=[vmem] * 3,
        out_specs=[hbm] * 2,
        scratch_shapes=[pltpu.VMEM((PANEL, PANEL), f32), pltpu.VMEM((ROWS, PANEL), f32), sems((STORES + 1,))],
        compiler_params=pltpu.CompilerParams(vmem_limit_bytes=16 << 20),
        name="solve",
    )(upper, inverse, total)


def solution(mesh):
    in_specs = (
        P(("user", "item"), None),
        P("user", "item", None),
        P("user", "item"),
        P("user", "item"),
    )
    out_specs = (P(), P("item", None))
    return jax.shard_map(
        on_device, mesh=mesh, in_specs=in_specs, out_specs=out_specs, check_vma=False
    )
```

```python
import jax
import jax.numpy as jnp
from jax import lax
from jax.sharding import PartitionSpec as P
import jax.experimental.pallas as pl
import jax.experimental.pallas.tpu as pltpu

BLOCK = 128
PANEL = 256
BLK_DEV = 8
ROWS = BLK_DEV * BLOCK
SIDE = 4
DEPTH = 16
SHARE = 16
TILE = 8
NB = 32
STORES = 4
PIECES = 4
MESH = pl.DeviceIdType.MESH
REACH = 4
NEAR_Z = (4, -4, 3, -3, 2, -2, 1, -1)
FAR_FIRST_XY = sorted(
    ((dy, dx) for dy in range(SIDE) for dx in range(SIDE) if dy or dx),
    key=lambda d: -(min(d[0], SIDE - d[0]) + min(d[1], SIDE - d[1])),
)
FAR_FIRST_SIDE = (2, 1, 3)
ORDER = (
    ("sum", 0), ("sum", 1), ("half", 0), ("sum", 2), ("diag", 0), ("factor", 0), ("sum", 3), ("pass", 0), ("factor", 1),
    ("pass", 1), ("factor", 2), ("pass", 2), ("factor", 3), ("pass", 3), ("factor", 4), ("factor", 5), ("factor", 6),
    ("factor", 7),
)


def split3(x):
    high = x.astype(jnp.bfloat16)
    rest = x - high.astype(jnp.float32)
    middle = rest.astype(jnp.bfloat16)
    low = (rest - middle.astype(jnp.float32)).astype(jnp.bfloat16)
    return high, middle, low


def eliminate(rows, inverse, start, count):
    left = rows.shape[0]
    columns = jnp.stack([jnp.broadcast_to(rows[:, start + t : start + t + 1], (left, BLOCK)) for t in range(count)])
    tile_sub = lax.broadcasted_iota(jnp.int32, (8, BLOCK), 0)
    rows_done, inverse_done, pivots = [], [], None
    for t in range(count):
        s = t % 8
        here = columns[0]
        pivots = jnp.where(tile_sub == s, here[:8], pivots) if s else here[:8]
        reciprocal = 1.0 / here[s : s + 1]
        below = jnp.where(lax.broadcasted_iota(jnp.int32, (left, BLOCK), 0) > s, here, 0.0)
        if t < count - 1:
            columns = columns[1:] - (below[None] * columns[1:, s : s + 1]) * reciprocal[None]
        scaled = below * reciprocal
        rows = rows - jnp.concatenate([scaled, scaled], 1) * rows[s : s + 1]
        inverse = inverse - scaled * inverse[s : s + 1]
        if s == 7:
            scale = lax.rsqrt(pivots)
            rows_done.append(rows[:8] * jnp.concatenate([scale, scale], 1))
            inverse_done.append(inverse[:8] * scale)
            left -= 8
            if left:
                rows, inverse, columns = rows[8:], inverse[8:], columns[:, 8:]
    return rows_done, inverse_done, rows, inverse


def factor_step(step, work_ref, upper_ref):
    start, stop = NB * step, NB * (step + 1)
    rows = work_ref[start:stop, :]
    lane = lax.broadcasted_iota(jnp.int32, (NB, BLOCK), 1)
    sub = lax.broadcasted_iota(jnp.int32, (NB, BLOCK), 0)
    inverse = jnp.where(lane == sub + start % BLOCK, 1.0, 0.0).astype(jnp.float32)
    rows1, inverse1, rows, inverse = eliminate(rows, inverse, start, NB // 2)
    rows2, inverse2, _, _ = eliminate(rows, inverse, start + NB // 2, NB // 2)
    upper = jnp.concatenate(rows1 + rows2, 0)
    inverse = jnp.concatenate(inverse1 + inverse2, 0)
    col = lax.broadcasted_iota(jnp.int32, (NB, PANEL), 1)
    row = lax.broadcasted_iota(jnp.int32, (NB, PANEL), 0)
    done = jnp.where((col >= start) & (col < stop), jnp.concatenate([inverse, inverse], 1), upper)
    upper_ref[start:stop, :] = jnp.where(col >= row + start, upper, 0.0)
    work_ref[start:stop, :] = jnp.where(col < stop, done, 0.0)
    if stop == PANEL:
        return
    base = BLOCK * (stop // BLOCK)
    dh, dm, dl = split3(done)
    ih, im, il = split3(upper[:, base:])
    product = lax.dot_general(
        jnp.concatenate([ih, ih, im, ih, im, il], 0),
        jnp.concatenate([dh, dm, dh, dl, dm, dh], 0),
        (((0,), (0,)), ((), ())),
        preferred_element_type=jnp.float32,
    )
    wide = lax.broadcasted_iota(jnp.int32, (PANEL - stop, PANEL), 1)
    kept = jnp.where((wide >= start) & (wide < stop), 0.0, work_ref[stop:, :])
    work_ref[stop:, :] = kept - product[stop - base :, :]


def gram_kernel(
    panel_ref, values_ref, list_ref, count_ref, upper_ref, work, total,
    users, values, turned, slot_list, diag, diag_in, part, in1, sum1, in2,
    load_sem, z_send, z_recv, f_send, f_recv, core_send, core_recv, ds_send, ds_recv, dg_send, dg_recv, half_sem,
    s1_send, s1_recv, s2_send, s2_recv, s3_send, s3_recv, s4_send, s4_recv,
):
    user = lax.axis_index("user")
    item = lax.axis_index("item")
    y, x = user // SIDE, user % SIDE
    z, core = item // 2, item % 2
    other = 1 - core

    def at_xy(dy, dx):
        return ((y + dy) % SIDE) * SIDE + (x + dx) % SIDE

    def at_z(d):
        return (z + DEPTH + d) % DEPTH

    z_ids = [(user, at_z(d) * 2 + core) for d in NEAR_Z]
    xy_ids = [(at_xy(*d), item) for d in FAR_FIRST_XY]
    core_id = (user, z * 2 + other)

    def remote(src, dst, send, recv, device):
        return pltpu.make_async_remote_copy(
            src_ref=src, dst_ref=dst, send_sem=send, recv_sem=recv, device_id=device, device_id_type=MESH
        )

    def start(copies):
        for copy in copies:
            copy.start()

    def wait(ref, sem):
        pltpu.make_async_copy(ref, ref, sem).wait()

    barrier = pltpu.get_barrier_semaphore()
    for device in z_ids + xy_ids + [core_id]:
        pl.semaphore_signal(barrier, inc=1, device_id=device, device_id_type=MESH)

    own_loads = [
        pltpu.make_async_copy(panel_ref.at[:, pl.ds(p * BLOCK, BLOCK)], users.at[p, core, z], load_sem.at[p])
        for p in range(2)
    ]
    loads = [pltpu.make_async_copy(list_ref, slot_list, load_sem.at[2])] + [
        pltpu.make_async_copy(values_ref.at[:, :, c], values.at[c, pl.ds(0, BLK_DEV - 1)], load_sem.at[3 + c])
        for c in range(2)
    ]
    start(own_loads + loads)
    for c in range(2):
        values[c, BLK_DEV - 1] = jnp.zeros((DEPTH, SHARE, BLOCK), jnp.bfloat16)
    for load in own_loads:
        load.wait()
    pl.semaphore_wait(barrier, len(z_ids) + len(xy_ids) + 1)

    z_copies = [
        [
            remote(users.at[p, core, z], users.at[p, core, z], z_send, z_recv.at[p, k], device)
            for k, device in enumerate(z_ids)
        ]
        for p in range(2)
    ]
    start(z_copies[0] + z_copies[1])

    def pass_to_core(p, place):
        return remote(users.at[p, core, place], users.at[p, core, place], core_send, core_recv.at[p], core_id)

    for p in range(2):
        pass_to_core(p, z).start()

    for load in loads:
        load.wait()
    used = count_ref[0, 0]
    for b in range(BLK_DEV):
        slot = jnp.int32(BLK_DEV - 1)
        for k in range(BLK_DEV - 1):
            slot = jnp.where((slot_list[0, k] == b) & (k < used), k, slot)
        for c in range(2):
            block = values[c, slot].reshape(DEPTH * SHARE, BLOCK)
            turned[pl.ds(b * BLOCK, BLOCK), pl.ds(c * DEPTH * SHARE, DEPTH * SHARE)] = block.T

    passed = ([], [])
    for p in range(2):
        for k, d in reversed(list(enumerate(NEAR_Z))):
            z_copies[p][k].wait_recv()
            came_from = at_z(-d)
            if d != -REACH:
                way = REACH if d > 0 else -REACH
                f = len(passed[p])
                piece_ref = users.at[p, core, came_from]
                copy = remote(piece_ref, piece_ref, f_send, f_recv.at[p, f], (user, at_z(way) * 2 + core))
                copy.start()
                passed[p].append((copy, at_z(-d - way)))
            pass_to_core(p, came_from).start()

    def finish_gather(p):
        for copy, came_from in passed[p]:
            copy.wait_recv()
            pass_to_core(p, came_from).start()
        wait(users.at[p, other], core_recv.at[p])
        return users[p].reshape(2 * DEPTH * SHARE, BLOCK)

    along = (
        [((at_xy(0, d), item), (x + d) % SIDE) for d in FAR_FIRST_SIDE],
        [((at_xy(d, 0), item), (y + d) % SIDE) for d in FAR_FIRST_SIDE],
    )
    place = (x, y)
    piece = ROWS // PIECES
    big, small = piece // SIDE, piece // SIDE**2

    def half_of(q):
        return 2 * q // PIECES

    def first_row(q, h):
        return h * (ROWS // 2) + (q % (PIECES // 2)) * piece

    def big_rows(q, h, i):
        return pl.ds(pl.multiple_of(first_row(q, h) + i * big, big), big)

    def small_rows(q, h, i):
        return pl.ds(pl.multiple_of(first_row(q, h) + i * small, small), small)

    def own_rows(q, h):
        return small_rows(q, h, place[h] * SIDE + place[1 - h])

    pairs = [(k, h) for k in range(SIDE - 1) for h in range(2)]
    s1 = [
        [
            remote(
                part.at[half_of(q), big_rows(q, h, along[h][k][1])], in1.at[q, h, k],
                s1_send, s1_recv.at[q], along[h][k][0],
            )
            for k, h in pairs
        ]
        for q in range(PIECES)
    ]
    s2 = [
        [
            remote(
                sum1.at[q, h, pl.ds(pl.multiple_of(along[1 - h][k][1] * small, small), small)], in2.at[q, h, k],
                s2_send, s2_recv.at[q], along[1 - h][k][0],
            )
            for k, h in pairs
        ]
        for q in range(PIECES)
    ]
    s3 = [
        [
            remote(
                total.at[half_of(q), own_rows(q, h)], total.at[half_of(q), own_rows(q, h)],
                s3_send, s3_recv.at[q], along[1 - h][k][0],
            )
            for k, h in pairs
        ]
        for q in range(PIECES)
    ]
    s4 = [
        [
            remote(
                total.at[half_of(q), big_rows(q, h, place[h])], total.at[half_of(q), big_rows(q, h, place[h])],
                s4_send, s4_recv.at[q], along[h][k][0],
            )
            for k, h in pairs
        ]
        for q in range(PIECES)
    ]

    def products(p, gathered):
        for q in range(p * PIECES // 2, (p + 1) * PIECES // 2):
            for h in range(2):
                rows = pl.ds(first_row(q, h), piece)
                part[p, rows, :] = jnp.dot(turned[rows, :], gathered, preferred_element_type=jnp.float32)
            start(s1[q])

    gathered0 = finish_gather(0)
    products(0, gathered0)
    gathered1 = finish_gather(1)

    def diag_rows(device_user):
        return pl.ds(pl.multiple_of((core * SIDE * SIDE + device_user) * TILE, TILE), TILE)

    gathered = jnp.concatenate([gathered0, gathered1], 1)
    diag[...] = lax.dot_general(
        gathered, gathered, (((0,), (0,)), ((), ())), preferred_element_type=jnp.float32
    )
    ds_copies = [remote(diag.at[diag_rows(d[0])], diag_in.at[user], ds_send, ds_recv, d) for d in xy_ids]
    start(ds_copies)
    diag_in[user] = diag[diag_rows(user), :]
    products(1, gathered1)

    others = diag_in.at[pl.ds(0, len(xy_ids))]
    wait(others, ds_recv)
    diag_sum = diag_in[0]
    for k in range(1, SIDE * SIDE):
        diag_sum = diag_sum + diag_in[k]
    row = lax.broadcasted_iota(jnp.int32, (TILE, PANEL), 0) + (core * SIDE * SIDE + user) * TILE
    col = lax.broadcasted_iota(jnp.int32, (TILE, PANEL), 1)
    work[diag_rows(user), :] = diag_sum + jnp.where(row == col, 0.5, 0.0)
    dg_copies = [
        remote(work.at[diag_rows(user)], work.at[diag_rows(user)], dg_send, dg_recv, d)
        for d in xy_ids
    ]
    start(dg_copies)
    core_half = pl.ds(pl.multiple_of(core * BLOCK, BLOCK), BLOCK)
    half_copy = remote(work.at[core_half], work.at[core_half], half_sem.at[0], half_sem.at[1], core_id)

    for q in range(PIECES):
        wait(in1.at[q], s1_recv.at[q])
        for h in range(2):
            sum1[q, h] = part[half_of(q), big_rows(q, h, place[h]), :] + in1[q, h, 0] + in1[q, h, 1] + in1[q, h, 2]
        start(s2[q])

    for what, n in ORDER:
        if what == "half":
            wait(others, dg_recv)
            wait(others, dg_send)
            half_copy.start()
        elif what == "diag":
            half_copy.wait()
        elif what == "factor":
            factor_step(n, work, upper_ref)
        elif what == "sum":
            wait(in2.at[n], s2_recv.at[n])
            for h in range(2):
                mine = sum1[n, h, pl.ds(pl.multiple_of(place[1 - h] * small, small), small), :]
                total[half_of(n), own_rows(n, h), :] = mine + in2[n, h, 0] + in2[n, h, 1] + in2[n, h, 2]
            start(s3[n])
        else:
            wait(in2.at[n], s3_recv.at[n])
            start(s4[n])
    for q in range(PIECES):
        wait(in1.at[q], s4_recv.at[q])
    wait(in1, s1_send)
    wait(in2, s2_send)
    wait(in2, s3_send)
    wait(in1, s4_send)
    wait(others, ds_send)
    wait(users.at[:, core], core_send)
    wait(users.at[:, core, pl.ds(0, 2 * REACH)], z_send)
    wait(users.at[:, core, pl.ds(0, 2 * REACH - 1)], f_send)


def solve_kernel(upper_ref, inverse_ref, total_ref, diag_out, below_out, lower, below, sem):
    stores = []
    for i in range(STORES):
        rows = pl.ds(i * (ROWS // STORES), ROWS // STORES)
        below[rows, :] = lax.dot_general(
            jnp.concatenate([total_ref[0, rows, :], total_ref[1, rows, :]], 1), inverse_ref[...],
            (((1,), (1,)), ((), ())),
            precision=lax.Precision.HIGHEST, preferred_element_type=jnp.float32,
        )
        stores.append(pltpu.make_async_copy(below.at[rows], below_out.at[rows], sem.at[i]))
        stores[-1].start()
    lower[...] = upper_ref[...].T
    stores.append(pltpu.make_async_copy(lower, diag_out, sem.at[STORES]))
    stores[-1].start()
    for store in stores:
        store.wait()


def on_device(panel_users, block_values, block_list, block_count):
    f32, bf16 = jnp.float32, jnp.bfloat16
    slots = block_values.shape[1]
    values = block_values.transpose(1, 0, 2).reshape(slots, DEPTH, 2, SHARE, BLOCK)
    vmem = pl.BlockSpec(memory_space=pltpu.VMEM)
    hbm = pl.BlockSpec(memory_space=pltpu.HBM)
    sems = pltpu.SemaphoreType.DMA
    big, small = ROWS // PIECES // SIDE, ROWS // PIECES // SIDE**2
    upper, inverse, total = pl.pallas_call(
        gram_kernel,
        out_shape=[
            pltpu.VMEM((PANEL, PANEL), f32),
            pltpu.VMEM((PANEL, PANEL), f32),
            pltpu.VMEM((2, ROWS, BLOCK), f32),
        ],
        in_specs=[hbm, hbm, hbm, pl.BlockSpec(memory_space=pltpu.SMEM)],
        out_specs=[vmem, vmem, vmem],
        scratch_shapes=[
            pltpu.VMEM((2, 2, DEPTH, SHARE, BLOCK), bf16),
            pltpu.VMEM((2, BLK_DEV, DEPTH, SHARE, BLOCK), bf16),
            pltpu.VMEM((ROWS, 2 * DEPTH * SHARE), bf16),
            pltpu.SMEM((1, slots), jnp.int32),
            pltpu.VMEM((PANEL, PANEL), f32),
            pltpu.VMEM((SIDE * SIDE, TILE, PANEL), f32),
            pltpu.VMEM((2, ROWS, BLOCK), f32),
            pltpu.VMEM((PIECES, 2, SIDE - 1, big, BLOCK), f32),
            pltpu.VMEM((PIECES, 2, big, BLOCK), f32),
            pltpu.VMEM((PIECES, 2, SIDE - 1, small, BLOCK), f32),
            sems((5,)),
            sems,
            sems((2, 2 * REACH)),
            sems,
            sems((2, 2 * REACH - 1)),
            sems,
            sems((2,)),
        ]
        + [sems] * 4
        + [sems((2,))]
        + [sems, sems((PIECES,))] * 4,
        compiler_params=pltpu.CompilerParams(
            collective_id=0, has_side_effects=True, vmem_limit_bytes=32 << 20
        ),
        name="gram",
    )(*[pltpu.with_memory_space_constraint(a, pltpu.HBM) for a in (panel_users, values, block_list)], block_count)
    return pl.pallas_call(
        solve_kernel,
        out_shape=[jax.ShapeDtypeStruct((PANEL, PANEL), f32), jax.ShapeDtypeStruct((ROWS, PANEL), f32)],
        in_specs=[vmem] * 3,
        out_specs=[hbm] * 2,
        scratch_shapes=[pltpu.VMEM((PANEL, PANEL), f32), pltpu.VMEM((ROWS, PANEL), f32), sems((STORES + 1,))],
        compiler_params=pltpu.CompilerParams(vmem_limit_bytes=16 << 20),
        name="solve",
    )(upper, inverse, total)


def solution(mesh):
    in_specs = (
        P(("user", "item"), None),
        P("user", "item", None),
        P("user", "item"),
        P("user", "item"),
    )
    out_specs = (P(), P("item", None))
    return jax.shard_map(
        on_device, mesh=mesh, in_specs=in_specs, out_specs=out_specs, check_vma=False
    )
```

```python
import jax
import jax.numpy as jnp
from jax import lax
from jax.sharding import PartitionSpec as P
import jax.experimental.pallas as pl
import jax.experimental.pallas.tpu as pltpu

BLOCK = 128
PANEL = 256
BLK_DEV = 8
ROWS = BLK_DEV * BLOCK
SIDE = 4
DEPTH = 16
SHARE = 16
TILE = 8
NB = 32
STORES = 4
PIECES = 4
MESH = pl.DeviceIdType.MESH
REACH = 4
NEAR_Z = (4, -4, 3, -3, 2, -2, 1, -1)
FAR_FIRST_XY = sorted(
    ((dy, dx) for dy in range(SIDE) for dx in range(SIDE) if dy or dx),
    key=lambda d: -(min(d[0], SIDE - d[0]) + min(d[1], SIDE - d[1])),
)
FAR_FIRST_SIDE = (2, 1, 3)
ORDER = (
    ("share", 0), ("first", 0), ("first", 1), ("first", 2), ("first", 3), ("sum", 0), ("half", 0), ("sum", 1), ("sum", 2),
    ("diag", 0), ("factor", 0), ("sum", 3), ("pass", 0), ("pass", 1), ("factor", 1), ("factor", 2), ("pass", 2), ("factor", 3),
    ("pass", 3), ("factor", 4), ("factor", 5), ("factor", 6), ("factor", 7),
)


def split3(x):
    high = x.astype(jnp.bfloat16)
    rest = x - high.astype(jnp.float32)
    middle = rest.astype(jnp.bfloat16)
    low = (rest - middle.astype(jnp.float32)).astype(jnp.bfloat16)
    return high, middle, low


def eliminate(rows, inverse, start, count):
    left = rows.shape[0]
    columns = jnp.stack([jnp.broadcast_to(rows[:, start + t : start + t + 1], (left, BLOCK)) for t in range(count)])
    tile_sub = lax.broadcasted_iota(jnp.int32, (8, BLOCK), 0)
    rows_done, inverse_done, pivots = [], [], None
    for t in range(count):
        s = t % 8
        here = columns[0]
        pivots = jnp.where(tile_sub == s, here[:8], pivots) if s else here[:8]
        reciprocal = 1.0 / here[s : s + 1]
        below = jnp.where(lax.broadcasted_iota(jnp.int32, (left, BLOCK), 0) > s, here, 0.0)
        if t < count - 1:
            columns = columns[1:] - (below[None] * columns[1:, s : s + 1]) * reciprocal[None]
        scaled = below * reciprocal
        rows = rows - jnp.concatenate([scaled, scaled], 1) * rows[s : s + 1]
        inverse = inverse - scaled * inverse[s : s + 1]
        if s == 7:
            scale = lax.rsqrt(pivots)
            rows_done.append(rows[:8] * jnp.concatenate([scale, scale], 1))
            inverse_done.append(inverse[:8] * scale)
            left -= 8
            if left:
                rows, inverse, columns = rows[8:], inverse[8:], columns[:, 8:]
    return rows_done, inverse_done, rows, inverse


def factor_step(step, work_ref, upper_ref):
    start, stop = NB * step, NB * (step + 1)
    rows = work_ref[start:stop, :]
    lane = lax.broadcasted_iota(jnp.int32, (NB, BLOCK), 1)
    sub = lax.broadcasted_iota(jnp.int32, (NB, BLOCK), 0)
    inverse = jnp.where(lane == sub + start % BLOCK, 1.0, 0.0).astype(jnp.float32)
    rows1, inverse1, rows, inverse = eliminate(rows, inverse, start, NB // 2)
    rows2, inverse2, _, _ = eliminate(rows, inverse, start + NB // 2, NB // 2)
    upper = jnp.concatenate(rows1 + rows2, 0)
    inverse = jnp.concatenate(inverse1 + inverse2, 0)
    col = lax.broadcasted_iota(jnp.int32, (NB, PANEL), 1)
    row = lax.broadcasted_iota(jnp.int32, (NB, PANEL), 0)
    done = jnp.where((col >= start) & (col < stop), jnp.concatenate([inverse, inverse], 1), upper)
    upper_ref[start:stop, :] = jnp.where(col >= row + start, upper, 0.0)
    work_ref[start:stop, :] = jnp.where(col < stop, done, 0.0)
    if stop == PANEL:
        return
    base = BLOCK * (stop // BLOCK)
    dh, dm, dl = split3(done)
    ih, im, il = split3(upper[:, base:])
    product = lax.dot_general(
        jnp.concatenate([ih, ih, im, ih, im, il], 0),
        jnp.concatenate([dh, dm, dh, dl, dm, dh], 0),
        (((0,), (0,)), ((), ())),
        preferred_element_type=jnp.float32,
    )
    wide = lax.broadcasted_iota(jnp.int32, (PANEL - stop, PANEL), 1)
    kept = jnp.where((wide >= start) & (wide < stop), 0.0, work_ref[stop:, :])
    work_ref[stop:, :] = kept - product[stop - base :, :]


def gram_kernel(
    panel_ref, values_ref, list_ref, count_ref, upper_ref, work, total,
    users, values, turned, slot_list, diag, diag_in, part, in1, sum1, in2,
    load_sem, z_send, z_recv, f_send, f_recv, core_send, core_recv, ds_send, ds_recv, dg_send, dg_recv, half_sem,
    s1_send, s1_recv, s2_send, s2_recv, s3_send, s3_recv, s4_send, s4_recv,
):
    user = lax.axis_index("user")
    item = lax.axis_index("item")
    y, x = user // SIDE, user % SIDE
    z, core = item // 2, item % 2
    other = 1 - core

    def at_xy(dy, dx):
        return ((y + dy) % SIDE) * SIDE + (x + dx) % SIDE

    def at_z(d):
        return (z + DEPTH + d) % DEPTH

    z_ids = [(user, at_z(d) * 2 + core) for d in NEAR_Z]
    xy_ids = [(at_xy(*d), item) for d in FAR_FIRST_XY]
    core_id = (user, z * 2 + other)

    def remote(src, dst, send, recv, device):
        return pltpu.make_async_remote_copy(
            src_ref=src, dst_ref=dst, send_sem=send, recv_sem=recv, device_id=device, device_id_type=MESH
        )

    def start(copies):
        for copy in copies:
            copy.start()

    def wait(ref, sem):
        pltpu.make_async_copy(ref, ref, sem).wait()

    barrier = pltpu.get_barrier_semaphore()
    for device in z_ids + xy_ids + [core_id]:
        pl.semaphore_signal(barrier, inc=1, device_id=device, device_id_type=MESH)

    own_loads = [
        pltpu.make_async_copy(panel_ref.at[:, pl.ds(p * BLOCK, BLOCK)], users.at[p, core, z], load_sem.at[p])
        for p in range(2)
    ]
    loads = [pltpu.make_async_copy(list_ref, slot_list, load_sem.at[2])] + [
        pltpu.make_async_copy(values_ref.at[:, :, c], values.at[c, pl.ds(0, BLK_DEV - 1)], load_sem.at[3 + c])
        for c in range(2)
    ]
    start(own_loads + loads)
    for c in range(2):
        values[c, BLK_DEV - 1] = jnp.zeros((DEPTH, SHARE, BLOCK), jnp.bfloat16)
    for load in own_loads:
        load.wait()
    pl.semaphore_wait(barrier, len(z_ids) + len(xy_ids) + 1)

    z_copies = [
        [
            remote(users.at[p, core, z], users.at[p, core, z], z_send, z_recv.at[p, k], device)
            for k, device in enumerate(z_ids)
        ]
        for p in range(2)
    ]
    start(z_copies[0] + z_copies[1])

    def pass_to_core(p, place):
        return remote(users.at[p, core, place], users.at[p, core, place], core_send, core_recv.at[p], core_id)

    for p in range(2):
        pass_to_core(p, z).start()

    for load in loads:
        load.wait()
    used = count_ref[0, 0]
    for b in range(BLK_DEV):
        slot = jnp.int32(BLK_DEV - 1)
        for k in range(BLK_DEV - 1):
            slot = jnp.where((slot_list[0, k] == b) & (k < used), k, slot)
        for c in range(2):
            block = values[c, slot].reshape(DEPTH * SHARE, BLOCK)
            turned[pl.ds(b * BLOCK, BLOCK), pl.ds(c * DEPTH * SHARE, DEPTH * SHARE)] = block.T

    passed = ([], [])
    for p in range(2):
        for k, d in reversed(list(enumerate(NEAR_Z))):
            z_copies[p][k].wait_recv()
            came_from = at_z(-d)
            if d != -REACH:
                way = REACH if d > 0 else -REACH
                f = len(passed[p])
                piece_ref = users.at[p, core, came_from]
                copy = remote(piece_ref, piece_ref, f_send, f_recv.at[p, f], (user, at_z(way) * 2 + core))
                copy.start()
                passed[p].append((copy, at_z(-d - way)))
            pass_to_core(p, came_from).start()

    def finish_gather(p):
        for copy, came_from in passed[p]:
            copy.wait_recv()
            pass_to_core(p, came_from).start()
        wait(users.at[p, other], core_recv.at[p])
        return users[p].reshape(2 * DEPTH * SHARE, BLOCK)

    along = (
        [((at_xy(0, d), item), (x + d) % SIDE) for d in FAR_FIRST_SIDE],
        [((at_xy(d, 0), item), (y + d) % SIDE) for d in FAR_FIRST_SIDE],
    )
    place = (x, y)
    piece = ROWS // PIECES
    big, small = piece // SIDE, piece // SIDE**2

    def half_of(q):
        return 2 * q // PIECES

    def first_row(q, h):
        return h * (ROWS // 2) + (q % (PIECES // 2)) * piece

    def big_rows(q, h, i):
        return pl.ds(pl.multiple_of(first_row(q, h) + i * big, big), big)

    def small_rows(q, h, i):
        return pl.ds(pl.multiple_of(first_row(q, h) + i * small, small), small)

    def own_rows(q, h):
        return small_rows(q, h, place[h] * SIDE + place[1 - h])

    pairs = [(k, h) for k in range(SIDE - 1) for h in range(2)]
    s1 = [
        [
            remote(
                part.at[half_of(q), big_rows(q, h, along[h][k][1])], in1.at[q, h, k],
                s1_send, s1_recv.at[q], along[h][k][0],
            )
            for k, h in pairs
        ]
        for q in range(PIECES)
    ]
    s2 = [
        [
            remote(
                sum1.at[q, h, pl.ds(pl.multiple_of(along[1 - h][k][1] * small, small), small)], in2.at[q, h, k],
                s2_send, s2_recv.at[q], along[1 - h][k][0],
            )
            for k, h in pairs
        ]
        for q in range(PIECES)
    ]
    s3 = [
        [
            remote(
                total.at[half_of(q), own_rows(q, h)], total.at[half_of(q), own_rows(q, h)],
                s3_send, s3_recv.at[q], along[1 - h][k][0],
            )
            for k, h in pairs
        ]
        for q in range(PIECES)
    ]
    s4 = [
        [
            remote(
                total.at[half_of(q), big_rows(q, h, place[h])], total.at[half_of(q), big_rows(q, h, place[h])],
                s4_send, s4_recv.at[q], along[h][k][0],
            )
            for k, h in pairs
        ]
        for q in range(PIECES)
    ]

    def products(p, gathered):
        for q in range(p * PIECES // 2, (p + 1) * PIECES // 2):
            for h in range(2):
                rows = pl.ds(first_row(q, h), piece)
                part[p, rows, :] = jnp.dot(turned[rows, :], gathered, preferred_element_type=jnp.float32)
            start(s1[q])

    gathered0 = finish_gather(0)
    products(0, gathered0)
    gathered1 = finish_gather(1)

    def diag_rows(device_user):
        return pl.ds(pl.multiple_of((core * SIDE * SIDE + device_user) * TILE, TILE), TILE)

    gathered = jnp.concatenate([gathered0, gathered1], 1)
    diag[...] = lax.dot_general(
        gathered, gathered, (((0,), (0,)), ((), ())), preferred_element_type=jnp.float32
    )
    ds_copies = [remote(diag.at[diag_rows(d[0])], diag_in.at[user], ds_send, ds_recv, d) for d in xy_ids]
    start(ds_copies)
    diag_in[user] = diag[diag_rows(user), :]
    products(1, gathered1)

    others = diag_in.at[pl.ds(0, len(xy_ids))]
    dg_copies = [remote(work.at[diag_rows(user)], work.at[diag_rows(user)], dg_send, dg_recv, d) for d in xy_ids]
    core_half = pl.ds(pl.multiple_of(core * BLOCK, BLOCK), BLOCK)
    half_copy = remote(work.at[core_half], work.at[core_half], half_sem.at[0], half_sem.at[1], core_id)

    for what, n in ORDER:
        if what == "first":
            wait(in1.at[n], s1_recv.at[n])
            for h in range(2):
                mine = part[half_of(n), big_rows(n, h, place[h]), :]
                sum1[n, h] = mine + in1[n, h, 0] + in1[n, h, 1] + in1[n, h, 2]
            start(s2[n])
        elif what == "share":
            wait(others, ds_recv)
            diag_sum = diag_in[0]
            for k in range(1, SIDE * SIDE):
                diag_sum = diag_sum + diag_in[k]
            row = lax.broadcasted_iota(jnp.int32, (TILE, PANEL), 0) + (core * SIDE * SIDE + user) * TILE
            col = lax.broadcasted_iota(jnp.int32, (TILE, PANEL), 1)
            work[diag_rows(user), :] = diag_sum + jnp.where(row == col, 0.5, 0.0)
            start(dg_copies)
        elif what == "half":
            wait(others, dg_recv)
            wait(others, dg_send)
            half_copy.start()
        elif what == "diag":
            half_copy.wait()
        elif what == "factor":
            factor_step(n, work, upper_ref)
        elif what == "sum":
            wait(in2.at[n], s2_recv.at[n])
            for h in range(2):
                mine = sum1[n, h, pl.ds(pl.multiple_of(place[1 - h] * small, small), small), :]
                total[half_of(n), own_rows(n, h), :] = mine + in2[n, h, 0] + in2[n, h, 1] + in2[n, h, 2]
            start(s3[n])
        else:
            wait(in2.at[n], s3_recv.at[n])
            start(s4[n])
    for q in range(PIECES):
        wait(in1.at[q], s4_recv.at[q])
    wait(in1, s1_send)
    wait(in2, s2_send)
    wait(in2, s3_send)
    wait(in1, s4_send)
    wait(others, ds_send)
    wait(users.at[:, core], core_send)
    wait(users.at[:, core, pl.ds(0, 2 * REACH)], z_send)
    wait(users.at[:, core, pl.ds(0, 2 * REACH - 1)], f_send)


def solve_kernel(upper_ref, inverse_ref, total_ref, diag_out, below_out, lower, below, sem):
    stores = []
    for i in range(STORES):
        rows = pl.ds(i * (ROWS // STORES), ROWS // STORES)
        below[rows, :] = lax.dot_general(
            jnp.concatenate([total_ref[0, rows, :], total_ref[1, rows, :]], 1), inverse_ref[...],
            (((1,), (1,)), ((), ())),
            precision=lax.Precision.HIGHEST, preferred_element_type=jnp.float32,
        )
        stores.append(pltpu.make_async_copy(below.at[rows], below_out.at[rows], sem.at[i]))
        stores[-1].start()
    lower[...] = upper_ref[...].T
    stores.append(pltpu.make_async_copy(lower, diag_out, sem.at[STORES]))
    stores[-1].start()
    for store in stores:
        store.wait()


def on_device(panel_users, block_values, block_list, block_count):
    f32, bf16 = jnp.float32, jnp.bfloat16
    slots = block_values.shape[1]
    values = block_values.transpose(1, 0, 2).reshape(slots, DEPTH, 2, SHARE, BLOCK)
    vmem = pl.BlockSpec(memory_space=pltpu.VMEM)
    hbm = pl.BlockSpec(memory_space=pltpu.HBM)
    sems = pltpu.SemaphoreType.DMA
    big, small = ROWS // PIECES // SIDE, ROWS // PIECES // SIDE**2
    upper, inverse, total = pl.pallas_call(
        gram_kernel,
        out_shape=[
            pltpu.VMEM((PANEL, PANEL), f32),
            pltpu.VMEM((PANEL, PANEL), f32),
            pltpu.VMEM((2, ROWS, BLOCK), f32),
        ],
        in_specs=[hbm, hbm, hbm, pl.BlockSpec(memory_space=pltpu.SMEM)],
        out_specs=[vmem, vmem, vmem],
        scratch_shapes=[
            pltpu.VMEM((2, 2, DEPTH, SHARE, BLOCK), bf16),
            pltpu.VMEM((2, BLK_DEV, DEPTH, SHARE, BLOCK), bf16),
            pltpu.VMEM((ROWS, 2 * DEPTH * SHARE), bf16),
            pltpu.SMEM((1, slots), jnp.int32),
            pltpu.VMEM((PANEL, PANEL), f32),
            pltpu.VMEM((SIDE * SIDE, TILE, PANEL), f32),
            pltpu.VMEM((2, ROWS, BLOCK), f32),
            pltpu.VMEM((PIECES, 2, SIDE - 1, big, BLOCK), f32),
            pltpu.VMEM((PIECES, 2, big, BLOCK), f32),
            pltpu.VMEM((PIECES, 2, SIDE - 1, small, BLOCK), f32),
            sems((5,)),
            sems,
            sems((2, 2 * REACH)),
            sems,
            sems((2, 2 * REACH - 1)),
            sems,
            sems((2,)),
        ]
        + [sems] * 4
        + [sems((2,))]
        + [sems, sems((PIECES,))] * 4,
        compiler_params=pltpu.CompilerParams(
            collective_id=0, has_side_effects=True, vmem_limit_bytes=32 << 20
        ),
        name="gram",
    )(*[pltpu.with_memory_space_constraint(a, pltpu.HBM) for a in (panel_users, values, block_list)], block_count)
    return pl.pallas_call(
        solve_kernel,
        out_shape=[jax.ShapeDtypeStruct((PANEL, PANEL), f32), jax.ShapeDtypeStruct((ROWS, PANEL), f32)],
        in_specs=[vmem] * 3,
        out_specs=[hbm] * 2,
        scratch_shapes=[pltpu.VMEM((PANEL, PANEL), f32), pltpu.VMEM((ROWS, PANEL), f32), sems((STORES + 1,))],
        compiler_params=pltpu.CompilerParams(vmem_limit_bytes=16 << 20),
        name="solve",
    )(upper, inverse, total)


def solution(mesh):
    in_specs = (
        P(("user", "item"), None),
        P("user", "item", None),
        P("user", "item"),
        P("user", "item"),
    )
    out_specs = (P(), P("item", None))
    return jax.shard_map(
        on_device, mesh=mesh, in_specs=in_specs, out_specs=out_specs, check_vma=False
    )
```
